256 devices in a mesh: loop: 32 (over y_lo, z, core), rep: 8 (over x, y_hi).
Axes of the slice: x: 4, y: 4 (y_hi: 2, y_lo: 2; y = y_hi * 2 + y_lo), z: 8, core: 2. Of those that a mesh axis runs over, the one named last changes fastest.
Arguments:
- ham_blocks: bfloat16 [256, 24, 128, 128], P('loop', 'rep'), may hold values from -0.109375 to 0.109375
- margin_blocks: bfloat16 [256, 24, 128, 128], P('loop', 'rep'), may hold values from -0.109375 to 0.109375
- block_cols: int32 [256, 24], P('loop'), may hold values from 0 to 255, as said below
- block_counts: int32 [256], P('loop'), may hold values from 12 to 24
- pert_real: bfloat16 [32768, 1024], P('loop', 'rep'), may hold values from -6 to 6
- pert_imag: bfloat16 [32768, 1024], P('loop', 'rep'), may hold values from -6 to 6
- drive_real: bfloat16 [32768, 1024], P('loop', 'rep'), may hold values from -6 to 6
- drive_imag: bfloat16 [32768, 1024], P('loop', 'rep'), may hold values from -6 to 6
Outputs:
- new_real: float32 [32768, 1024], P('loop', 'rep')
- new_imag: float32 [32768, 1024], P('loop', 'rep')
The draws below stay inside these ranges and needn't reach their ends.
Inputs may be any that keep to these rules, and one draw needn't show every extreme that they name: `block_cols`: the 24 entries of a row are distinct block columns.
All inputs are finite; a program needn't handle non-finite values.
Results may differ from the reference program's by a relative error of at most 0.0003.
Values may be sent and summed in bfloat16 or wider, within the bound.
No kernel may reach another device: no remote copies, remote signals or barrier semaphores. Data moves between devices by JAX's collectives and lax.ppermute only.
A program may use at most 128 MiB of HBM per device.

```python
import jax
import jax.numpy as jnp
from jax import lax

BLK = 128
KMAX = 24
NB = 256
ORDER = 32768
COLS = 1024


def draw_block_cols(key, part):
    key = jax.random.fold_in(key, 11)
    scores = jax.random.randint(key, (NB, NB), 0, 2 ** 20) * NB + jnp.arange(NB, dtype=jnp.int32)[None, :]
    order = jnp.argsort(scores, axis=1, stable=True)
    return order[:, :KMAX].astype(jnp.int32)


def draw_block_counts(key, part):
    key = jax.random.fold_in(key, 23)
    counts = jax.random.randint(key, (NB,), KMAX // 2, KMAX + 1)
    counts = counts.at[0].set(KMAX).at[1].set(KMAX // 2)
    return counts.astype(jnp.int32)


def steps_of(stream_key, shape, split, least, top_value):
    def one(dim, shards_of):
        heights = jax.random.uniform(jax.random.fold_in(jax.random.fold_in(stream_key, 6), dim), (shards_of,), jnp.float32, least / len(split), top_value / len(split))
        return jnp.repeat(jnp.exp(heights), shape[dim] // shards_of).reshape((-1,) + (1,) * (len(shape) - dim - 1))

    level = one(*split[0])
    for cut in split[1:]:
        level = level * one(*cut)
    return level


def normal_values(stream_key, dims, scale, most, pieces=(), held_as=jnp.bfloat16):
    result = jax.random.normal(stream_key, dims, jnp.float32) * scale
    if len(pieces) > 0:
        result = steps_of(stream_key, dims, pieces, -0.22, 0.18) * result
    return jnp.clip(result, min=-most, max=most).astype(held_as)


def setup_inputs(seed: int = 0) -> dict:
    key_list = jax.random.split(jax.random.key(seed), 9)
    ham_blocks = normal_values(key_list[0], (NB, KMAX, BLK, BLK), (KMAX * BLK) ** -0.5, 0.109375, ((0, 32), (1, 8)))
    margin_blocks = normal_values(key_list[1], (NB, KMAX, BLK, BLK), (KMAX * BLK) ** -0.5, 0.109375, ((0, 32), (1, 8)))
    block_cols = draw_block_cols(jax.random.fold_in(key_list[8], 71), 0)
    block_counts = draw_block_counts(jax.random.fold_in(key_list[8], 71), 0)
    pert_real = normal_values(key_list[4], (ORDER, COLS), 1.0, 6.0, ((0, 32), (1, 8)))
    pert_imag = normal_values(key_list[5], (ORDER, COLS), 1.0, 6.0, ((0, 32), (1, 8)))
    drive_real = normal_values(key_list[6], (ORDER, COLS), 1.0, 6.0, ((0, 32), (1, 8)))
    drive_imag = normal_values(key_list[7], (ORDER, COLS), 1.0, 6.0, ((0, 32), (1, 8)))
    return {"ham_blocks": ham_blocks, "margin_blocks": margin_blocks, "block_cols": block_cols, "block_counts": block_counts, "pert_real": pert_real, "pert_imag": pert_imag, "drive_real": drive_real, "drive_imag": drive_imag}


frequency = 0.7
damping = 0.5
step_length = 0.5


def reference(ham_blocks, margin_blocks, block_cols, block_counts, pert_real, pert_imag, drive_real, drive_imag):
    panels = jnp.concatenate([pert_real, pert_imag], axis=1).reshape(NB, BLK, 2 * COLS)

    def one_row(items):
        ham_row, margin_row, cols, count = items
        live = (jnp.arange(KMAX, dtype=jnp.int32) < count).astype(jnp.float32)
        picked = panels[cols].astype(jnp.float32)
        ham_live = ham_row.astype(jnp.float32) * live[:, None, None]
        margin_live = margin_row.astype(jnp.float32) * live[:, None, None]
        ham_term = jnp.einsum('kab,kbn->an', ham_live, picked)
        margin_term = jnp.einsum('kab,kbn->an', margin_live, picked)
        return ham_term, margin_term

    ham_prod, margin_prod = lax.map(one_row, (ham_blocks, margin_blocks, block_cols, block_counts))
    ham_prod = ham_prod.reshape(ORDER, 2 * COLS)
    margin_prod = margin_prod.reshape(ORDER, 2 * COLS)
    ham_real, ham_imag = ham_prod[:, :COLS], ham_prod[:, COLS:]
    ovl_real, ovl_imag = margin_prod[:, :COLS], margin_prod[:, COLS:]
    res_real = drive_real.astype(jnp.float32) - (ham_real - frequency * ovl_real + damping * ovl_imag)
    res_imag = drive_imag.astype(jnp.float32) - (ham_imag - frequency * ovl_imag - damping * ovl_real)
    new_real = pert_real.astype(jnp.float32) + step_length * res_real
    new_imag = pert_imag.astype(jnp.float32) + step_length * res_imag
    return new_real, new_imag
```

```python
import functools

import jax
import jax.numpy as jnp
from jax import lax
from jax.experimental import pallas as pl
from jax.experimental.pallas import tpu as pltpu
from jax.sharding import PartitionSpec as P

frequency = 0.7
damping = 0.5
step_length = 0.5

AXES = ("ylo", "z", "core", "x", "yhi")
SIZES = (2, 8, 2, 4, 2)
BLOCK = 128


def moves(axis, by):
    place = AXES.index(axis)
    stride = 1
    for size in SIZES[place + 1 :]:
        stride *= size
    total = 1
    for size in SIZES:
        total *= size
    pairs = []
    for source in range(total):
        at = source // stride % SIZES[place]
        pairs.append((source, source + ((at + by) % SIZES[place] - at) * stride))
    return pairs


def shift(array, axis, by=1):
    return lax.ppermute(array, AXES, moves(axis, by))


def slot_list():
    out = []
    for j in range(3):
        out.append(("own", j, 0, 0, j))
    for j in range(3):
        out.append(("from_left", j, 3, 0, j))
    for j in range(3):
        out.append(("from_right", j, 1, 0, j))
    for j in range(3):
        out.append(("far", j, 2, 0, j))
    for j in range(3):
        out.append(("part", j, 0, 1, j))
    for j in range(2):
        out.append(("part_left", j, 3, 1, j))
    for j in range(2):
        out.append(("part_right", j, 1, 1, j))
    for j in range(2):
        out.append(("part_far", j, 2, 1, j))
    out.append(("late", 0, 3, 1, 2))
    out.append(("late", 1, 1, 1, 2))
    out.append(("late_far", 0, 2, 1, 2))
    return out


def product_kernel(
    half,
    last,
    place_ref,
    cols_ref,
    counts_ref,
    *refs,
):
    refs = list(refs)
    panel_own, panel_other = refs[:2]
    pieces = {
        "own": refs[2],
        "from_left": refs[3],
        "from_right": refs[4],
        "far": (refs[5], refs[6]),
        "part": refs[7],
        "part_left": refs[8],
        "part_right": refs[9],
        "part_far": (refs[10], refs[11]),
        "late": refs[12],
        "late_far": refs[13],
    }
    if last:
        before, pert_real, pert_imag, drive_real, drive_imag = refs[14:19]
        new_real, new_imag, panel, sems = refs[19:]
    else:
        acc_out, panel, sems = refs[14:]
    row = pl.program_id(0)
    count = panel_own.shape[0]
    my_ylo, my_core, my_x, my_yhi = (place_ref[n] for n in range(4))

    @pl.when(row == 0)
    def _():
        copies = [
            pltpu.make_async_copy(panel_own, panel.at[pl.ds(my_core * count, count)], sems.at[0]),
            pltpu.make_async_copy(panel_other, panel.at[pl.ds((1 - my_core) * count, count)], sems.at[1]),
        ]
        for copy in copies:
            copy.start()
        for copy in copies:
            copy.wait()

    slots = slot_list()
    total = None
    for first in range(0, 24, 8):
        left, right = [], []
        for name, position, dx, dy, j in slots[first : first + 8]:
            ref = pieces[name]
            if isinstance(ref, tuple):
                top, bottom = ref[0][0, position], ref[1][0, position]
            else:
                top, bottom = ref[0, 0, position], ref[1, 0, position]
            left.append(jnp.concatenate([top, bottom], axis=0))
            slot = 3 * (2 * ((my_x + dx) & 3) + (my_yhi ^ dy)) + j
            column = cols_ref[row, slot]
            owner = column >> 3
            use = (slot < counts_ref[row]) & (((owner >> 4) ^ my_ylo) == half)
            block = panel[(owner & 1) * count + ((owner >> 1) & 7) * 8 + (column & 7)]
            right.append(jnp.where(use, block, jnp.zeros_like(block)))
        term = jnp.dot(
            jnp.concatenate(left, axis=1),
            jnp.concatenate(right, axis=0),
            preferred_element_type=jnp.float32,
        )
        total = term if total is None else total + term
    if not last:
        acc_out[0] = total
        return
    total = total + before[0]
    ham_real, ham_imag = total[:BLOCK, :BLOCK], total[:BLOCK, BLOCK:]
    ovl_real, ovl_imag = total[BLOCK:, :BLOCK], total[BLOCK:, BLOCK:]
    res_real = drive_real[...].astype(jnp.float32) - (
        ham_real - frequency * ovl_real + damping * ovl_imag
    )
    res_imag = drive_imag[...].astype(jnp.float32) - (
        ham_imag - frequency * ovl_imag - damping * ovl_real
    )
    new_real[...] = pert_real[...].astype(jnp.float32) + step_length * res_real
    new_imag[...] = pert_imag[...].astype(jnp.float32) + step_length * res_imag


def products(half, place, cols, counts, panel_own, panel_other, pieces, tail=None):
    last = tail is not None
    rows = cols.shape[0]
    whole = pl.BlockSpec(memory_space=pl.ANY)

    def by_row(array):
        if array.ndim == 5:
            n = array.shape[2]
            return pl.BlockSpec((2, 1, n, BLOCK, BLOCK), lambda i, *_: (0, i, 0, 0, 0))
        n = array.shape[1]
        return pl.BlockSpec((1, n, BLOCK, BLOCK), lambda i, *_: (i, 0, 0, 0))

    acc_spec = pl.BlockSpec((1, 2 * BLOCK, 2 * BLOCK), lambda i, *_: (i, 0, 0))
    flat_spec = pl.BlockSpec((BLOCK, BLOCK), lambda i, *_: (i, 0))
    in_specs = [whole, whole] + [by_row(a) for a in pieces]
    args = [panel_own, panel_other] + list(pieces)
    if last:
        in_specs += [acc_spec] + [flat_spec] * 4
        args += list(tail)
        out_specs = [flat_spec] * 2
        out_shape = [jax.ShapeDtypeStruct((rows * BLOCK, BLOCK), jnp.float32)] * 2
    else:
        out_specs = acc_spec
        out_shape = jax.ShapeDtypeStruct((rows, 2 * BLOCK, 2 * BLOCK), jnp.float32)
    return pl.pallas_call(
        functools.partial(product_kernel, half, last),
        grid_spec=pltpu.PrefetchScalarGridSpec(
            num_scalar_prefetch=3,
            grid=(rows,),
            in_specs=in_specs,
            out_specs=out_specs,
            scratch_shapes=[
                pltpu.VMEM((2 * panel_own.shape[0], BLOCK, 2 * BLOCK), jnp.bfloat16),
                pltpu.SemaphoreType.DMA((2,)),
            ],
        ),
        out_shape=out_shape,
        compiler_params=pltpu.CompilerParams(vmem_limit_bytes=40 * 2**20),
        cost_estimate=pl.CostEstimate(
            flops=2 * rows * 24 * 2 * BLOCK * BLOCK * 2 * BLOCK,
            bytes_accessed=22 * 2**20,
            transcendentals=0,
        ),
        name="products_last" if last else "products_first",
    )(place, cols, counts, *args)


def per_device(
    ham_blocks,
    margin_blocks,
    block_cols,
    block_counts,
    pert_real,
    pert_imag,
    drive_real,
    drive_imag,
):
    rows = block_cols.shape[0]
    place = jnp.stack([lax.axis_index(a) for a in ("ylo", "core", "x", "yhi")]).astype(jnp.int32)

    panel = jnp.concatenate([pert_real, pert_imag], axis=1).reshape(rows, BLOCK, 2 * BLOCK)
    both = jnp.stack([ham_blocks, margin_blocks], axis=0)

    near = lax.all_gather(panel, "z", axis=0, tiled=True)
    neighbour = shift(panel, "ylo")
    from_left = shift(both, "x", 1)
    from_right = shift(both, "x", -1)
    part = shift(both, "yhi")
    far = lax.all_gather(neighbour, "z", axis=0, tiled=True)
    near_other = shift(near, "core")

    far_ham = shift(from_left[0], "x", 1)
    far_margin = shift(from_right[1], "x", -1)
    late = shift(jnp.concatenate([from_left[:, :, 2:], from_right[:, :, 2:]], axis=2), "yhi")
    part_two = part[:, :, :2]
    part_left = shift(part_two, "x", 1)
    part_right = shift(part_two, "x", -1)
    late_far = shift(jnp.stack([far_ham[:, 2:], far_margin[:, 2:]], axis=0), "yhi")
    part_far_ham = shift(part_left[0], "x", 1)
    part_far_margin = shift(part_right[1], "x", -1)
    far_other = shift(far, "core")

    pieces = (
        both,
        from_left,
        from_right,
        far_ham,
        far_margin,
        part,
        part_left,
        part_right,
        part_far_ham,
        part_far_margin,
        late,
        late_far,
    )
    before = products(0, place, block_cols, block_counts, near, near_other, pieces)
    new_real, new_imag = products(
        1,
        place,
        block_cols,
        block_counts,
        far,
        far_other,
        pieces,
        (before, pert_real, pert_imag, drive_real, drive_imag),
    )
    return new_real, new_imag


def solution(mesh):
    fine = jax.sharding.Mesh(mesh.devices.reshape(SIZES), AXES)
    loop, rep = ("ylo", "z", "core"), ("x", "yhi")
    return jax.shard_map(
        per_device,
        mesh=fine,
        in_specs=(
            P(loop, rep, None, None),
            P(loop, rep, None, None),
            P(loop, None),
            P(loop),
            P(loop, rep),
            P(loop, rep),
            P(loop, rep),
            P(loop, rep),
        ),
        out_specs=(P(loop, rep), P(loop, rep)),
        check_vma=False,
    )
```

```python
import jax
import jax.numpy as jnp
from jax import lax
from jax.experimental import pallas as pl
from jax.experimental.pallas import tpu as pltpu
from jax.sharding import PartitionSpec as P

frequency = 0.7
damping = 0.5
step_length = 0.5

AXES = ("ylo", "z", "core", "x", "yhi")
SIZES = (2, 8, 2, 4, 2)
BLOCK = 128


def moves(axis, by):
    place = AXES.index(axis)
    stride = 1
    for size in SIZES[place + 1 :]:
        stride *= size
    total = 1
    for size in SIZES:
        total *= size
    pairs = []
    for source in range(total):
        at = source // stride % SIZES[place]
        pairs.append((source, source + ((at + by) % SIZES[place] - at) * stride))
    return pairs


def shift(array, axis, by=1):
    return lax.ppermute(array, AXES, moves(axis, by))


PIECES = (
    (0, 0, (0, 1, 2)),
    (3, 0, (0, 1, 2)),
    (1, 0, (0, 1, 2)),
    (2, 0, (0, 1, 2)),
    (0, 1, (0, 1, 2)),
    (3, 1, (0, 1)),
    (1, 1, (0, 1)),
    (2, 1, (0, 1)),
    (3, 1, (2,)),
    (1, 1, (2,)),
    (2, 1, (2,)),
)
GROUP = 4


def list_kernel(place_ref, cols_ref, counts_ref, order_ref, used_ref):
    rows, slots = cols_ref.shape
    my_ylo, my_core, my_x, my_yhi = (place_ref[n] for n in range(4))

    def one_row(row, carry):
        for which in range(2):
            used_ref[which, row] = 0
            for n in range(order_ref.shape[2]):
                order_ref[which, row, n] = 0
        place = 0
        for dx, dy, local in PIECES:
            for j in local:
                slot = 3 * (2 * ((my_x + dx) & 3) + (my_yhi ^ dy)) + j
                column = cols_ref[row, slot]
                owner = column >> 3
                far = (owner >> 4) ^ my_ylo
                other = (owner & 1) ^ my_core
                which = far * other
                at = ((owner >> 1) & 7) * 8 + (column & 7) + (1 - which) * (2 * far + other) * 64

                @pl.when(slot < counts_ref[row])
                def _(which=which, at=at, place=place):
                    n = used_ref[which, row]
                    order_ref[which, row, n] = place * 256 + at
                    used_ref[which, row] = n + 1

                place += 1
        return carry

    lax.fori_loop(0, rows, one_row, 0)


def make_lists(place, cols, counts):
    rows = cols.shape[0]
    smem = pl.BlockSpec(memory_space=pltpu.SMEM)
    return pl.pallas_call(
        list_kernel,
        in_specs=[smem] * 3,
        out_specs=[smem] * 2,
        out_shape=[
            jax.ShapeDtypeStruct((2, rows, 24 + GROUP), jnp.int32),
            jax.ShapeDtypeStruct((2, rows), jnp.int32),
        ],
        name="make_lists",
    )(place, cols, counts)


def add_products(which, order_ref, used_ref, blocks, panel, acc, fresh):
    def one_row(row, carry):
        used = used_ref[which, row]
        if fresh:
            acc[row] = jnp.zeros(acc.shape[1:], acc.dtype)

        def one_group(group, carry):
            left, right = [], []
            for n in range(GROUP):
                code = order_ref[which, row, group * GROUP + n]
                place, at = code >> 8, code & 255
                left.append(jnp.concatenate([blocks[0, place, row], blocks[1, place, row]], axis=0))
                block = panel[at]
                right.append(jnp.where(group * GROUP + n < used, block, jnp.zeros_like(block)))
            acc[row] += jnp.dot(
                jnp.concatenate(left, axis=1),
                jnp.concatenate(right, axis=0),
                preferred_element_type=jnp.float32,
            )
            return carry

        return lax.fori_loop(0, (used + GROUP - 1) // GROUP, one_group, carry)

    lax.fori_loop(0, used_ref.shape[1], one_row, 0)


def fetch(pairs, sems):
    copies = [pltpu.make_async_copy(a, b, sems.at[n]) for n, (a, b) in enumerate(pairs)]
    for copy in copies:
        copy.start()
    for copy in copies:
        copy.wait()


def first_kernel(order_ref, used_ref, near, near_other, far, *refs):
    pieces, (blocks, acc, panel, sems) = refs[:12], refs[12:]
    count = near.shape[0]
    pairs = [(ref, panel.at[pl.ds(n * count, count)]) for n, ref in enumerate((near, near_other, far))]
    at = 0
    for n, piece in enumerate(pieces):
        if n in (4, 9):
            continue
        if n in (3, 8):
            size = piece.shape[0]
            pairs.append((piece, blocks.at[0, pl.ds(at, size)]))
            pairs.append((pieces[n + 1], blocks.at[1, pl.ds(at, size)]))
        else:
            size = piece.shape[1]
            pairs.append((piece, blocks.at[:, pl.ds(at, size)]))
        at += size
    fetch(pairs, sems)
    add_products(0, order_ref, used_ref, blocks, panel, acc, True)


def last_kernel(
    order_ref,
    used_ref,
    far_other,
    blocks,
    before,
    pert_real,
    pert_imag,
    drive_real,
    drive_imag,
    new_real,
    new_imag,
    acc,
    panel,
    sems,
):
    fetch([(far_other, panel)], sems)
    acc[...] = before[...]
    add_products(1, order_ref, used_ref, blocks, panel, acc, False)

    def one_row(row, carry):
        total = acc[row]
        lines = pl.ds(row * BLOCK, BLOCK)
        ham_real, ham_imag = total[:BLOCK, :BLOCK], total[:BLOCK, BLOCK:]
        ovl_real, ovl_imag = total[BLOCK:, :BLOCK], total[BLOCK:, BLOCK:]
        res_real = drive_real[lines].astype(jnp.float32) - (
            ham_real - frequency * ovl_real + damping * ovl_imag
        )
        res_imag = drive_imag[lines].astype(jnp.float32) - (
            ham_imag - frequency * ovl_imag - damping * ovl_real
        )
        new_real[lines] = pert_real[lines].astype(jnp.float32) + step_length * res_real
        new_imag[lines] = pert_imag[lines].astype(jnp.float32) + step_length * res_imag
        return carry

    lax.fori_loop(0, acc.shape[0], one_row, 0)


SMEM = pl.BlockSpec(memory_space=pltpu.SMEM)
VMEM = pl.BlockSpec(memory_space=pltpu.VMEM)
ANY = pl.BlockSpec(memory_space=pl.ANY)


def nothing(*refs):
    pass


def after(array, *others):
    return pl.pallas_call(
        nothing,
        in_specs=[ANY] * (1 + len(others)),
        out_specs=ANY,
        out_shape=jax.ShapeDtypeStruct(array.shape, array.dtype),
        input_output_aliases={0: 0},
        compiler_params=pltpu.CompilerParams(vmem_limit_bytes=2**16),
        name="gate",
    )(in_hbm(array), *map(in_hbm, others))


def in_hbm(array):
    return pltpu.with_memory_space_constraint(array, pltpu.HBM)


def held(array):
    return pltpu.with_memory_space_constraint(array, pltpu.VMEM)


def cost(micros):
    return pl.CostEstimate(flops=0, bytes_accessed=int(micros * 3.0e6), transcendentals=0)


def first_products(order, used, near, near_other, far, pieces):
    rows, count = used.shape[1], near.shape[0]
    return pl.pallas_call(
        first_kernel,
        in_specs=[SMEM, SMEM] + [ANY] * (3 + len(pieces)),
        out_specs=[VMEM, VMEM],
        out_shape=[
            pltpu.VMEM((2, 24, rows, BLOCK, BLOCK), jnp.bfloat16),
            pltpu.VMEM((rows, 2 * BLOCK, 2 * BLOCK), jnp.float32),
        ],
        scratch_shapes=[
            pltpu.VMEM((3 * count, BLOCK, 2 * BLOCK), jnp.bfloat16),
            pltpu.SemaphoreType.DMA((3 + len(pieces),)),
        ],
        compiler_params=pltpu.CompilerParams(vmem_limit_bytes=FIRST_LIMIT),
        cost_estimate=cost(10),
        name="products_first",
    )(order, used, in_hbm(near), in_hbm(near_other), in_hbm(far), *map(in_hbm, pieces))


def last_products(order, used, far_other, blocks, before, *flat):
    rows = used.shape[1]
    return pl.pallas_call(
        last_kernel,
        in_specs=[SMEM, SMEM, ANY, VMEM, VMEM] + [VMEM] * 4,
        out_specs=[VMEM] * 2,
        out_shape=[jax.ShapeDtypeStruct((rows * BLOCK, BLOCK), jnp.float32)] * 2,
        scratch_shapes=[
            pltpu.VMEM(before.shape, jnp.float32),
            pltpu.VMEM(far_other.shape, far_other.dtype),
            pltpu.SemaphoreType.DMA((1,)),
        ],
        compiler_params=pltpu.CompilerParams(vmem_limit_bytes=LATER_LIMIT),
        cost_estimate=cost(4),
        name="products_last",
    )(order, used, far_other, held(blocks), held(before), *flat)


FIRST_LIMIT = 15 * 2**20
LATER_LIMIT = 9 * 2**20


def per_device(
    ham_blocks,
    margin_blocks,
    block_cols,
    block_counts,
    pert_real,
    pert_imag,
    drive_real,
    drive_imag,
):
    rows = block_cols.shape[0]
    place = jnp.stack([lax.axis_index(a) for a in ("ylo", "core", "x", "yhi")]).astype(jnp.int32)

    both = jnp.stack([ham_blocks.swapaxes(0, 1), margin_blocks.swapaxes(0, 1)], axis=0)
    panel = jnp.concatenate([pert_real, pert_imag], axis=1).reshape(rows, BLOCK, 2 * BLOCK)

    from_left = shift(both, "x", 1)
    from_right = shift(both, "x", -1)
    part = shift(both, "yhi")
    near = lax.all_gather(panel, "z", axis=0, tiled=True)
    order, used = make_lists(place, block_cols, block_counts)

    neighbour = shift(panel, "ylo")
    far = lax.all_gather(after(neighbour, from_left, from_right, part, order), "z", axis=0, tiled=True)
    far_ham = shift(from_left[0], "x", 1)
    far_margin = shift(from_right[1], "x", -1)
    late = shift(jnp.concatenate([from_left[:, 2:], from_right[:, 2:]], axis=1), "yhi")

    part_two = after(part[:, :2], far_ham, far_margin)
    part_left = shift(part_two, "x", 1)
    part_right = shift(part_two, "x", -1)
    near = after(near, far_ham, far_margin, late)
    near_other = shift(near, "core")
    late_far = shift(jnp.stack([far_ham[2:], far_margin[2:]], axis=0), "yhi")
    part_far_ham = shift(part_left[0], "x", 1)
    part_far_margin = shift(part_right[1], "x", -1)

    pieces = (
        both,
        from_left,
        from_right,
        far_ham,
        far_margin,
        part,
        part_left,
        part_right,
        part_far_ham,
        part_far_margin,
        late,
        late_far,
    )
    far = after(far, part_far_ham, part_far_margin, late_far)
    far_other = shift(far, "core")
    blocks, acc = first_products(order, used, near, near_other, far, pieces)
    new_real, new_imag = last_products(
        order, used, far_other, blocks, acc, pert_real, pert_imag, drive_real, drive_imag
    )
    return new_real, new_imag


def solution(mesh):
    fine = jax.sharding.Mesh(mesh.devices.reshape(SIZES), AXES)
    loop, rep = ("ylo", "z", "core"), ("x", "yhi")
    return jax.shard_map(
        per_device,
        mesh=fine,
        in_specs=(
            P(loop, rep, None, None),
            P(loop, rep, None, None),
            P(loop, None),
            P(loop),
            P(loop, rep),
            P(loop, rep),
            P(loop, rep),
            P(loop, rep),
        ),
        out_specs=(P(loop, rep), P(loop, rep)),
        check_vma=False,
    )
```

```python
import jax
import jax.numpy as jnp
from jax import lax
from jax.experimental import pallas as pl
from jax.experimental.pallas import tpu as pltpu
from jax.sharding import PartitionSpec as P

frequency = 0.7
damping = 0.5
step_length = 0.5

AXES = ("ylo", "z", "core", "x", "yhi")
SIZES = (2, 8, 2, 4, 2)
BLOCK = 128


def moves(axis, by):
    place = AXES.index(axis)
    stride = 1
    for size in SIZES[place + 1 :]:
        stride *= size
    total = 1
    for size in SIZES:
        total *= size
    pairs = []
    for source in range(total):
        at = source // stride % SIZES[place]
        pairs.append((source, source + ((at + by) % SIZES[place] - at) * stride))
    return pairs


def shift(array, axis, by=1):
    return lax.ppermute(array, AXES, moves(axis, by))


PIECES = (
    (0, 0, (0, 1, 2)),
    (3, 0, (0, 1, 2)),
    (1, 0, (0, 1, 2)),
    (2, 0, (0, 1, 2)),
    (0, 1, (0, 1)),
    (3, 1, (0, 1)),
    (1, 1, (0, 1)),
    (2, 1, (0, 1)),
    (0, 1, (2,)),
    (3, 1, (2,)),
    (1, 1, (2,)),
    (2, 1, (2,)),
)
STEP = 4
SKIP = 2**16


def list_kernel(place_ref, cols_ref, counts_ref, order_ref, row_ref, pairs_ref):
    rows, slots = cols_ref.shape
    my_ylo, my_core, my_x, my_yhi = (place_ref[n] for n in range(4))

    def one_row(row, ends):
        for which in range(3):
            pairs_ref[which] = ends[which]
        place = 0
        for dx, dy, local in PIECES:
            for j in local:
                slot = 3 * (2 * ((my_x + dx) & 3) + (my_yhi ^ dy)) + j
                column = cols_ref[row, slot]
                owner = column >> 3
                far = (owner >> 4) ^ my_ylo
                other = (owner & 1) ^ my_core
                which = far * (1 + other)
                at = ((owner >> 1) & 7) * 8 + (column & 7) + (1 - far) * other * 64

                @pl.when(slot < counts_ref[row])
                def _(which=which, at=at, place=place):
                    n = pairs_ref[which]
                    order_ref[which, n] = place * 256 + at
                    row_ref[which, n >> 1] = row
                    pairs_ref[which] = n + 1

                place += 1
        out = []
        for which in range(3):
            n = pairs_ref[which]
            order_ref[which, n] = SKIP
            out.append((n + 1) & ~1)
        return tuple(out)

    ends = lax.fori_loop(0, rows, one_row, (0, 0, 0))
    for which in range(3):
        for n in range(2 * STEP):
            order_ref[which, ends[which] + n] = SKIP
        for n in range(STEP):
            row_ref[which, (ends[which] >> 1) + n] = rows - 1
        pairs_ref[which] = ends[which] >> 1


def make_lists(place, cols, counts):
    most = cols.shape[0] * 24
    return pl.pallas_call(
        list_kernel,
        in_specs=[SMEM] * 3,
        out_specs=[SMEM] * 3,
        out_shape=[
            jax.ShapeDtypeStruct((3, most + 2 * STEP), jnp.int32),
            jax.ShapeDtypeStruct((3, most // 2 + STEP), jnp.int32),
            jax.ShapeDtypeStruct((3,), jnp.int32),
        ],
        name="make_lists",
    )(place, cols, counts)


def add_products(which, lists, blocks, panel, acc):
    order_ref, row_ref, pairs_ref = lists

    def one_step(step, carry):
        terms = []
        for pair in range(STEP):
            left, right = [], []
            for n in range(2):
                code = order_ref[which, (step * STEP + pair) * 2 + n]
                place, at = (code >> 8) & 31, code & 255
                row = row_ref[which, step * STEP + pair]
                left.append(jnp.concatenate([blocks[0, place, row], blocks[1, place, row]], axis=0))
                block = panel[at]
                right.append(jnp.where(code < SKIP, block, jnp.zeros_like(block)))
            terms.append(
                jnp.dot(
                    jnp.concatenate(left, axis=1),
                    jnp.concatenate(right, axis=0),
                    preferred_element_type=jnp.float32,
                )
            )
        for pair, term in enumerate(terms):
            acc[row_ref[which, step * STEP + pair]] += term
        return carry

    lax.fori_loop(0, (pairs_ref[which] + STEP - 1) // STEP, one_step, 0)


def fetch(pairs, sems):
    copies = [pltpu.make_async_copy(a, b, sems.at[n]) for n, (a, b) in enumerate(pairs)]
    for copy in copies:
        copy.start()
    for copy in copies:
        copy.wait()


def split_pieces(pieces, blocks):
    pairs, at = [], 0
    for piece in pieces:
        if isinstance(piece, tuple):
            size = piece[0].shape[0]
            pairs += [(piece[n], blocks.at[n, pl.ds(at, size)]) for n in range(2)]
        else:
            size = piece.shape[1]
            pairs.append((piece, blocks.at[:, pl.ds(at, size)]))
        at += size
    return pairs


def group_pieces(refs):
    return [*refs[:3], (refs[3], refs[4]), *refs[5:8], (refs[8], refs[9]), *refs[10:12]]


def near_kernel(order_ref, row_ref, pairs_ref, near, near_other, *refs):
    pieces, (acc, blocks, panel, sems) = refs[:12], refs[12:]
    count = near.shape[0]
    pairs = [(ref, panel.at[pl.ds(n * count, count)]) for n, ref in enumerate((near, near_other))]
    fetch(pairs + split_pieces(group_pieces(pieces), blocks), sems)
    acc[...] = jnp.zeros_like(acc)
    add_products(0, (order_ref, row_ref, pairs_ref), blocks, panel, acc)


def far_kernel(order_ref, row_ref, pairs_ref, far, before, *refs):
    pieces, (blocks, acc, panel, sems) = refs[:12], refs[12:]
    fetch([(far, panel), (before, acc)] + split_pieces(group_pieces(pieces), blocks), sems)
    add_products(1, (order_ref, row_ref, pairs_ref), blocks, panel, acc)


def last_kernel(
    order_ref,
    row_ref,
    pairs_ref,
    panel,
    blocks,
    before,
    pert_real,
    pert_imag,
    drive_real,
    drive_imag,
    new_real,
    new_imag,
    acc,
):
    acc[...] = before[...]
    add_products(2, (order_ref, row_ref, pairs_ref), blocks, panel, acc)

    def one_row(row, carry):
        total = acc[row]
        lines = pl.ds(row * BLOCK, BLOCK)
        ham_real, ham_imag = total[:BLOCK, :BLOCK], total[:BLOCK, BLOCK:]
        ovl_real, ovl_imag = total[BLOCK:, :BLOCK], total[BLOCK:, BLOCK:]
        res_real = drive_real[lines].astype(jnp.float32) - (
            ham_real - frequency * ovl_real + damping * ovl_imag
        )
        res_imag = drive_imag[lines].astype(jnp.float32) - (
            ham_imag - frequency * ovl_imag - damping * ovl_real
        )
        new_real[lines] = pert_real[lines].astype(jnp.float32) + step_length * res_real
        new_imag[lines] = pert_imag[lines].astype(jnp.float32) + step_length * res_imag
        return carry

    lax.fori_loop(0, acc.shape[0], one_row, 0)


SMEM = pl.BlockSpec(memory_space=pltpu.SMEM)
VMEM = pl.BlockSpec(memory_space=pltpu.VMEM)
ANY = pl.BlockSpec(memory_space=pl.ANY)


def nothing(*refs):
    pass


def after(array, *others):
    return pl.pallas_call(
        nothing,
        in_specs=[ANY] * (1 + len(others)),
        out_specs=ANY,
        out_shape=jax.ShapeDtypeStruct(array.shape, array.dtype),
        input_output_aliases={0: 0},
        compiler_params=pltpu.CompilerParams(vmem_limit_bytes=2**16),
        name="gate",
    )(in_hbm(array), *map(in_hbm, others))


def in_hbm(array):
    return pltpu.with_memory_space_constraint(array, pltpu.HBM)


def held(array):
    return pltpu.with_memory_space_constraint(array, pltpu.VMEM)


def cost(micros):
    return pl.CostEstimate(flops=0, bytes_accessed=int(micros * 3.0e6), transcendentals=0)


def near_products(lists, rows, near, near_other, pieces):
    count = near.shape[0]
    return pl.pallas_call(
        near_kernel,
        in_specs=[SMEM] * 3 + [ANY] * (2 + len(pieces)),
        out_specs=VMEM,
        out_shape=jax.ShapeDtypeStruct((rows, 2 * BLOCK, 2 * BLOCK), jnp.float32),
        scratch_shapes=[
            pltpu.VMEM((2, 24, rows, BLOCK, BLOCK), jnp.bfloat16),
            pltpu.VMEM((2 * count, BLOCK, 2 * BLOCK), jnp.bfloat16),
            pltpu.SemaphoreType.DMA((2 + len(pieces),)),
        ],
        compiler_params=pltpu.CompilerParams(vmem_limit_bytes=30 * 2**20),
        cost_estimate=cost(10),
        name="products_near",
    )(*lists, in_hbm(near), in_hbm(near_other), *map(in_hbm, pieces))


def far_products(lists, far, before, pieces):
    rows = before.shape[0]
    return pl.pallas_call(
        far_kernel,
        in_specs=[SMEM] * 3 + [ANY] * (2 + len(pieces)),
        out_specs=[VMEM, VMEM],
        out_shape=[
            pltpu.VMEM((2, 24, rows, BLOCK, BLOCK), jnp.bfloat16),
            pltpu.VMEM(before.shape, jnp.float32),
        ],
        scratch_shapes=[
            pltpu.VMEM(far.shape, jnp.bfloat16),
            pltpu.SemaphoreType.DMA((2 + len(pieces),)),
        ],
        compiler_params=pltpu.CompilerParams(vmem_limit_bytes=7 * 2**20),
        cost_estimate=cost(8),
        name="products_far",
    )(*lists, in_hbm(far), in_hbm(before), *map(in_hbm, pieces))


def last_products(lists, far_other, blocks, before, *flat):
    rows = before.shape[0]
    return pl.pallas_call(
        last_kernel,
        in_specs=[SMEM] * 3 + [VMEM] * 7,
        out_specs=[VMEM] * 2,
        out_shape=[jax.ShapeDtypeStruct((rows * BLOCK, BLOCK), jnp.float32)] * 2,
        scratch_shapes=[pltpu.VMEM(before.shape, jnp.float32)],
        compiler_params=pltpu.CompilerParams(vmem_limit_bytes=7 * 2**20),
        cost_estimate=cost(4),
        name="products_last",
    )(*lists, held(far_other), held(blocks), held(before), *flat)


def per_device(
    ham_blocks,
    margin_blocks,
    block_cols,
    block_counts,
    pert_real,
    pert_imag,
    drive_real,
    drive_imag,
):
    rows = block_cols.shape[0]
    place = jnp.stack([lax.axis_index(a) for a in ("ylo", "core", "x", "yhi")]).astype(jnp.int32)

    both = jnp.stack([ham_blocks.swapaxes(0, 1), margin_blocks.swapaxes(0, 1)], axis=0)
    panel = jnp.concatenate([pert_real, pert_imag], axis=1).reshape(rows, BLOCK, 2 * BLOCK)

    from_left = shift(both, "x", 1)
    from_right = shift(both, "x", -1)
    part = shift(both[:, :2], "yhi")
    near = lax.all_gather(panel, "z", axis=0, tiled=True)
    lists = make_lists(place, block_cols, block_counts)
    neighbour = shift(panel, "ylo")

    far = lax.all_gather(after(neighbour, from_left, from_right, part, *lists), "z", axis=0, tiled=True)
    far_ham = shift(from_left[0], "x", 1)
    far_margin = shift(from_right[1], "x", -1)
    part_left = shift(part, "x", 1)
    part_right = shift(part, "x", -1)
    late = shift(
        jnp.concatenate([both[:, 2:], from_left[:, 2:], from_right[:, 2:]], axis=1), "yhi"
    )

    near = after(near, far_ham, far_margin, part_left, part_right, late)
    near_other = shift(near, "core")
    late_far = shift(jnp.stack([far_ham[2:], far_margin[2:]], axis=0), "yhi")
    part_far_ham = shift(part_left[0], "x", 1)
    part_far_margin = shift(part_right[1], "x", -1)

    pieces = (
        both,
        from_left,
        from_right,
        far_ham,
        far_margin,
        part,
        part_left,
        part_right,
        part_far_ham,
        part_far_margin,
        late,
        late_far,
    )
    acc = near_products(lists, rows, near, near_other, pieces)
    far = after(far, acc)
    far_other = shift(far, "core")
    blocks, acc = far_products(lists, far, acc, pieces)
    new_real, new_imag = last_products(
        lists, far_other, blocks, acc, pert_real, pert_imag, drive_real, drive_imag
    )
    return new_real, new_imag


def solution(mesh):
    fine = jax.sharding.Mesh(mesh.devices.reshape(SIZES), AXES)
    loop, rep = ("ylo", "z", "core"), ("x", "yhi")
    return jax.shard_map(
        per_device,
        mesh=fine,
        in_specs=(
            P(loop, rep, None, None),
            P(loop, rep, None, None),
            P(loop, None),
            P(loop),
            P(loop, rep),
            P(loop, rep),
            P(loop, rep),
            P(loop, rep),
        ),
        out_specs=(P(loop, rep), P(loop, rep)),
        check_vma=False,
    )
```

```python
import jax
import jax.numpy as jnp
from jax import lax
from jax.experimental import pallas as pl
from jax.experimental.pallas import tpu as pltpu
from jax.sharding import PartitionSpec as P

frequency = 0.7
damping = 0.5
step_length = 0.5

AXES = ("ylo", "z", "core", "x", "yhi")
SIZES = (2, 8, 2, 4, 2)
BLOCK = 128


def moves(axis, by):
    place = AXES.index(axis)
    stride = 1
    for size in SIZES[place + 1 :]:
        stride *= size
    total = 1
    for size in SIZES:
        total *= size
    pairs = []
    for source in range(total):
        at = source // stride % SIZES[place]
        pairs.append((source, source + ((at + by) % SIZES[place] - at) * stride))
    return pairs


def shift(array, axis, by=1):
    return lax.ppermute(array, AXES, moves(axis, by))


PIECES = (
    (0, 0, (0, 1, 2)),
    (3, 0, (0, 1, 2)),
    (1, 0, (0, 1, 2)),
    (2, 0, (0, 1, 2)),
    (0, 1, (0, 1)),
    (3, 1, (0, 1)),
    (1, 1, (0, 1)),
    (2, 1, (0, 1)),
    (0, 1, (2,)),
    (3, 1, (2,)),
    (1, 1, (2,)),
    (2, 1, (2,)),
)
STEP = 4
EARLY = 18
SKIP = 2**16


def list_kernel(place_ref, cols_ref, counts_ref, order_ref, row_ref, pairs_ref):
    rows, slots = cols_ref.shape
    my_ylo, my_z, my_core, my_x, my_yhi = (place_ref[n] for n in range(5))

    def one_row(row, ends):
        for which in range(3):
            pairs_ref[which] = ends[which]
        place = 0
        for dx, dy, local in PIECES:
            for j in local:
                slot = 3 * (2 * ((my_x + dx) & 3) + (my_yhi ^ dy)) + j
                column = cols_ref[row, slot]
                owner = column >> 3
                far = (owner >> 4) ^ my_ylo
                other = (owner & 1) ^ my_core
                ahead = ((owner >> 1) - my_z) & 7
                turn = jnp.where(ahead < 4, 2 * ahead, 15 - 2 * ahead)
                last = far & (turn + 2 * other >= 7).astype(jnp.int32)
                which = 2 * last + (1 - last) * (far | int(place >= EARLY))
                at = jnp.where(
                    far == 0,
                    (owner & 15) * 8,
                    jnp.where(
                        last == 1, other * (turn - 4) * 8, 128 + 56 * other + turn * 8
                    ),
                ) + (column & 7)

                @pl.when(slot < counts_ref[row])
                def _(which=which, at=at, place=place):
                    n = pairs_ref[which]
                    order_ref[which, n] = place * 256 + at
                    row_ref[which, n >> 1] = row
                    pairs_ref[which] = n + 1

                place += 1
        out = []
        for which in range(3):
            n = pairs_ref[which]
            order_ref[which, n] = SKIP
            out.append((n + 1) & ~1)
        return tuple(out)

    ends = lax.fori_loop(0, rows // 2, one_row, (0, 0, 0))
    for which in range(3):
        pairs_ref[3 + which] = ends[which] >> 1
    ends = lax.fori_loop(rows // 2, rows, one_row, ends)
    for which in range(3):
        for n in range(2 * STEP):
            order_ref[which, ends[which] + n] = SKIP
        for n in range(STEP):
            row_ref[which, (ends[which] >> 1) + n] = rows - 1
        pairs_ref[which] = ends[which] >> 1


def make_lists(place, cols, counts):
    most = cols.shape[0] * 24
    return pl.pallas_call(
        list_kernel,
        in_specs=[SMEM] * 3,
        out_specs=[SMEM] * 3,
        out_shape=[
            jax.ShapeDtypeStruct((3, most + 2 * STEP), jnp.int32),
            jax.ShapeDtypeStruct((3, most // 2 + STEP), jnp.int32),
            jax.ShapeDtypeStruct((6,), jnp.int32),
        ],
        name="make_lists",
    )(place, cols, counts)


def add_products(which, lists, blocks, panel, acc, first, end):
    order_ref, row_ref, pairs_ref = lists

    def one_step(step, carry):
        terms = []
        for pair in range(STEP):
            left, right = [], []
            for n in range(2):
                code = order_ref[which, (step * STEP + pair) * 2 + n]
                place, at = (code >> 8) & 31, code & 255
                row = row_ref[which, step * STEP + pair]
                left.append(jnp.concatenate([blocks[0, place, row], blocks[1, place, row]], axis=0))
                block = panel[at]
                right.append(jnp.where(code < SKIP, block, jnp.zeros_like(block)))
            terms.append(
                jnp.dot(
                    jnp.concatenate(left, axis=1),
                    jnp.concatenate(right, axis=0),
                    preferred_element_type=jnp.float32,
                )
            )
        for pair, term in enumerate(terms):
            acc[row_ref[which, step * STEP + pair]] += term
        return carry

    lax.fori_loop(first, end, one_step, 0)


def all_steps(which, lists):
    return (lists[2][which] + STEP - 1) // STEP


def run(which, lists, panel_parts, pieces, panel, blocks, acc, before, sems):
    half = blocks.shape[2] // 2
    early, at = [], 0
    for part in panel_parts:
        early.append((part, panel.at[pl.ds(at, part.shape[0])]))
        at += part.shape[0]
    if before is not None:
        early.append((before, acc))
    rounds = [early + split_pieces(pieces, blocks, 0, half), split_pieces(pieces, blocks, half, half)]
    copies, used = [], 0
    for pairs in rounds:
        copies.append([pltpu.make_async_copy(a, b, sems.at[used + n]) for n, (a, b) in enumerate(pairs)])
        used += len(pairs)
    for copy in copies[0] + copies[1]:
        copy.start()
    if before is None:
        acc[...] = jnp.zeros_like(acc)
    for copy in copies[0]:
        copy.wait()
    middle = lists[2][3 + which] // STEP
    add_products(which, lists, blocks, panel, acc, 0, middle)
    for copy in copies[1]:
        copy.wait()
    add_products(which, lists, blocks, panel, acc, middle, all_steps(which, lists))


def split_pieces(pieces, blocks, first, rows):
    pairs, at = [], 0
    lines = pl.ds(first, rows)
    for piece in pieces:
        if isinstance(piece, tuple):
            size = piece[0].shape[0]
            pairs += [(piece[n].at[:, lines], blocks.at[n, pl.ds(at, size), lines]) for n in range(2)]
        else:
            size = piece.shape[1]
            pairs.append((piece.at[:, :, lines], blocks.at[:, pl.ds(at, size), lines]))
        at += size
    return pairs


def group_pieces(refs):
    out = [*refs[:3], (refs[3], refs[4]), *refs[5:8]]
    if len(refs) > 8:
        out += [(refs[8], refs[9]), *refs[10:12]]
    return out


def early_kernel(order_ref, row_ref, pairs_ref, near, *refs):
    pieces, (acc, blocks, panel, sems) = refs[:8], refs[8:]
    lists = (order_ref, row_ref, pairs_ref)
    run(0, lists, [near], group_pieces(pieces), panel, blocks, acc, None, sems)


def main_kernel(order_ref, row_ref, pairs_ref, *refs):
    parts, before, pieces = refs[:9], refs[9], refs[10:22]
    blocks, acc, panel, sems = refs[22:]
    lists = (order_ref, row_ref, pairs_ref)
    run(1, lists, parts, group_pieces(pieces), panel, blocks, acc, before, sems)


def last_kernel(
    order_ref,
    row_ref,
    pairs_ref,
    end_up,
    end_down,
    other_third,
    other_end,
    blocks,
    before,
    pert_real,
    pert_imag,
    drive_real,
    drive_imag,
    new_real,
    new_imag,
    acc,
    panel,
    sems,
):
    copies, at = [], 0
    for n, part in enumerate((end_up, end_down, other_third, other_end)):
        copies.append(pltpu.make_async_copy(part, panel.at[pl.ds(at, part.shape[0])], sems.at[n]))
        at += part.shape[0]
    for copy in copies:
        copy.start()
    acc[...] = before[...]
    for copy in copies:
        copy.wait()
    lists = (order_ref, row_ref, pairs_ref)
    add_products(2, lists, blocks, panel, acc, 0, all_steps(2, lists))

    def one_row(row, carry):
        total = acc[row]
        lines = pl.ds(row * BLOCK, BLOCK)
        ham_real, ham_imag = total[:BLOCK, :BLOCK], total[:BLOCK, BLOCK:]
        ovl_real, ovl_imag = total[BLOCK:, :BLOCK], total[BLOCK:, BLOCK:]
        res_real = drive_real[lines].astype(jnp.float32) - (
            ham_real - frequency * ovl_real + damping * ovl_imag
        )
        res_imag = drive_imag[lines].astype(jnp.float32) - (
            ham_imag - frequency * ovl_imag - damping * ovl_real
        )
        new_real[lines] = pert_real[lines].astype(jnp.float32) + step_length * res_real
        new_imag[lines] = pert_imag[lines].astype(jnp.float32) + step_length * res_imag
        return carry

    lax.fori_loop(0, acc.shape[0], one_row, 0)


SMEM = pl.BlockSpec(memory_space=pltpu.SMEM)
VMEM = pl.BlockSpec(memory_space=pltpu.VMEM)
ANY = pl.BlockSpec(memory_space=pl.ANY)


def nothing(*refs):
    pass


def after(array, *others):
    return pl.pallas_call(
        nothing,
        in_specs=[ANY] * (1 + len(others)),
        out_specs=ANY,
        out_shape=jax.ShapeDtypeStruct(array.shape, array.dtype),
        input_output_aliases={0: 0},
        compiler_params=pltpu.CompilerParams(vmem_limit_bytes=2**16),
        name="gate",
    )(in_hbm(array), *map(in_hbm, others))


def in_hbm(array):
    return pltpu.with_memory_space_constraint(array, pltpu.HBM)


def held(array):
    return pltpu.with_memory_space_constraint(array, pltpu.VMEM)


def cost(micros):
    return pl.CostEstimate(flops=0, bytes_accessed=int(micros * 3.0e6), transcendentals=0)


def early_products(lists, rows, near, pieces):
    return pl.pallas_call(
        early_kernel,
        in_specs=[SMEM] * 3 + [ANY] * (1 + len(pieces)),
        out_specs=VMEM,
        out_shape=jax.ShapeDtypeStruct((rows, 2 * BLOCK, 2 * BLOCK), jnp.float32),
        scratch_shapes=[
            pltpu.VMEM((2, EARLY, rows, BLOCK, BLOCK), jnp.bfloat16),
            pltpu.VMEM(near.shape, jnp.bfloat16),
            pltpu.SemaphoreType.DMA((1 + 2 * len(pieces),)),
        ],
        compiler_params=pltpu.CompilerParams(vmem_limit_bytes=24 * 2**20),
        cost_estimate=cost(10),
        name="products_early",
    )(*lists, in_hbm(near), *map(in_hbm, pieces))


def main_products(lists, parts, before, pieces):
    rows = before.shape[0]
    return pl.pallas_call(
        main_kernel,
        in_specs=[SMEM] * 3 + [ANY] * (len(parts) + 1 + len(pieces)),
        out_specs=[VMEM, VMEM],
        out_shape=[
            pltpu.VMEM((2, 24, rows, BLOCK, BLOCK), jnp.bfloat16),
            pltpu.VMEM(before.shape, jnp.float32),
        ],
        scratch_shapes=[
            pltpu.VMEM((sum(a.shape[0] for a in parts), BLOCK, 2 * BLOCK), jnp.bfloat16),
            pltpu.SemaphoreType.DMA((len(parts) + 1 + 2 * len(pieces),)),
        ],
        compiler_params=pltpu.CompilerParams(vmem_limit_bytes=17 * 2**20),
        cost_estimate=cost(10),
        name="products_main",
    )(*lists, *map(in_hbm, parts), in_hbm(before), *map(in_hbm, pieces))


def last_products(lists, parts, blocks, before, *flat):
    rows = before.shape[0]
    return pl.pallas_call(
        last_kernel,
        in_specs=[SMEM] * 3 + [ANY] * 4 + [VMEM] * 6,
        out_specs=[VMEM] * 2,
        out_shape=[jax.ShapeDtypeStruct((rows * BLOCK, BLOCK), jnp.float32)] * 2,
        scratch_shapes=[
            pltpu.VMEM(before.shape, jnp.float32),
            pltpu.VMEM((sum(a.shape[0] for a in parts), BLOCK, 2 * BLOCK), jnp.bfloat16),
            pltpu.SemaphoreType.DMA((4,)),
        ],
        compiler_params=pltpu.CompilerParams(vmem_limit_bytes=9 * 2**20),
        cost_estimate=cost(4),
        name="products_last",
    )(*lists, *parts, held(blocks), held(before), *flat)


def per_device(
    ham_blocks,
    margin_blocks,
    block_cols,
    block_counts,
    pert_real,
    pert_imag,
    drive_real,
    drive_imag,
):
    rows = block_cols.shape[0]
    place = jnp.stack([lax.axis_index(a) for a in ("ylo", "z", "core", "x", "yhi")]).astype(jnp.int32)

    both = jnp.stack([ham_blocks.swapaxes(0, 1), margin_blocks.swapaxes(0, 1)], axis=0)
    panel = jnp.concatenate([pert_real, pert_imag], axis=1).reshape(rows, BLOCK, 2 * BLOCK)

    near = lax.all_gather(panel, ("z", "core"), axis=0, tiled=True)
    from_left = shift(both, "x", 1)
    from_right = shift(both, "x", -1)
    part = shift(both[:, :2], "yhi")
    neighbour = shift(panel, "ylo")
    lists = make_lists(place, block_cols, block_counts)
    up1, down1 = shift(neighbour, "z", 1), shift(neighbour, "z", -1)

    far_ham = shift(from_left[0], "x", 1)
    far_margin = shift(from_right[1], "x", -1)
    late = shift(
        after(jnp.concatenate([both[:, 2:], from_left[:, 2:], from_right[:, 2:]], axis=1), part),
        "yhi",
    )
    up2, down2 = shift(up1, "z", 1), shift(down1, "z", -1)

    part = after(part, far_ham, far_margin, lists[0])
    part_left = shift(part, "x", 1)
    part_right = shift(part, "x", -1)
    up3, down3 = shift(up2, "z", 1), shift(down2, "z", -1)
    late_far = shift(
        after(jnp.stack([far_ham[2:], far_margin[2:]], axis=0), late, part_left, part_right), "yhi"
    )
    part_far_ham = shift(part_left[0], "x", 1)
    part_far_margin = shift(part_right[1], "x", -1)
    up4, down4 = shift(up3[: rows // 2], "z", 1), shift(down3[rows // 2 :], "z", -1)

    early = (both, from_left, from_right, far_ham, far_margin, part, part_left, part_right)
    acc = early_products(lists, rows, near, early)
    other_first = shift(
        after(
            jnp.concatenate([neighbour, up1, down1, up2, down2], axis=0),
            up3,
            down3,
            late_far,
            part_far_ham,
            part_far_margin,
            acc,
        ),
        "core",
    )
    other_third = shift(jnp.concatenate([up3, down3], axis=0), "core")
    other_end = shift(jnp.concatenate([up4, down4], axis=0), "core")

    pieces = early + (part_far_ham, part_far_margin, late, late_far)
    parts = (near, neighbour, up1, down1, up2, down2, up3, down3, other_first)
    blocks, acc = main_products(lists, parts, acc, pieces)
    new_real, new_imag = last_products(
        lists,
        (up4, down4, other_third, other_end),
        blocks,
        acc,
        pert_real,
        pert_imag,
        drive_real,
        drive_imag,
    )
    return new_real, new_imag


def solution(mesh):
    fine = jax.sharding.Mesh(mesh.devices.reshape(SIZES), AXES)
    loop, rep = ("ylo", "z", "core"), ("x", "yhi")
    return jax.shard_map(
        per_device,
        mesh=fine,
        in_specs=(
            P(loop, rep, None, None),
            P(loop, rep, None, None),
            P(loop, None),
            P(loop),
            P(loop, rep),
            P(loop, rep),
            P(loop, rep),
            P(loop, rep),
        ),
        out_specs=(P(loop, rep), P(loop, rep)),
        check_vma=False,
    )
```

```python
import jax
import jax.numpy as jnp
from jax import lax
from jax.experimental import pallas as pl
from jax.experimental.pallas import tpu as pltpu
from jax.sharding import PartitionSpec as P

frequency = 0.7
damping = 0.5
step_length = 0.5

AXES = ("ylo", "z", "core", "x", "yhi")
SIZES = (2, 8, 2, 4, 2)
BLOCK = 128


def moves(axis, by):
    place = AXES.index(axis)
    stride = 1
    for size in SIZES[place + 1 :]:
        stride *= size
    total = 1
    for size in SIZES:
        total *= size
    pairs = []
    for source in range(total):
        at = source // stride % SIZES[place]
        pairs.append((source, source + ((at + by) % SIZES[place] - at) * stride))
    return pairs


def shift(array, axis, by=1):
    return lax.ppermute(array, AXES, moves(axis, by))


PIECES = (
    (0, 0, (0, 1, 2)),
    (3, 0, (0, 1, 2)),
    (1, 0, (0, 1, 2)),
    (2, 0, (0, 1, 2)),
    (0, 1, (0, 1)),
    (3, 1, (0, 1)),
    (1, 1, (0, 1)),
    (2, 1, (0, 1)),
    (0, 1, (2,)),
    (3, 1, (2,)),
    (1, 1, (2,)),
    (2, 1, (2,)),
)
STEP = 4
EARLY = 18
LISTS = 3
SKIP = 2**16


def list_kernel(place_ref, cols_ref, counts_ref, order_ref, row_ref, pairs_ref):
    rows, slots = cols_ref.shape
    my_ylo, my_core, my_x, my_yhi = (place_ref[n] for n in range(4))

    def one_row(row, ends):
        for which in range(LISTS):
            pairs_ref[which] = ends[which]
        place = 0
        for dx, dy, local in PIECES:
            for j in local:
                slot = 3 * (2 * ((my_x + dx) & 3) + (my_yhi ^ dy)) + j
                column = cols_ref[row, slot]
                owner = column >> 3
                far = (owner >> 4) ^ my_ylo
                other = (owner & 1) ^ my_core
                which = far * (1 + other) + (1 - far) * int(place >= EARLY)
                at = ((owner >> 1) & 7) * 8 + (column & 7) + (1 - (which >> 1)) * (2 * far + other) * 64

                @pl.when(slot < counts_ref[row])
                def _(which=which, at=at, place=place):
                    n = pairs_ref[which]
                    order_ref[which, n] = place * 256 + at
                    row_ref[which, n >> 1] = row
                    pairs_ref[which] = n + 1

                place += 1
        out = []
        for which in range(LISTS):
            n = pairs_ref[which]
            order_ref[which, n] = SKIP
            out.append((n + 1) & ~1)
        return tuple(out)

    ends = lax.fori_loop(0, rows // 2, one_row, (0,) * LISTS)
    for which in range(LISTS):
        pairs_ref[LISTS + which] = ends[which] >> 1
    ends = lax.fori_loop(rows // 2, rows, one_row, ends)
    for which in range(LISTS):
        for n in range(2 * STEP):
            order_ref[which, ends[which] + n] = SKIP
        for n in range(STEP):
            row_ref[which, (ends[which] >> 1) + n] = rows - 1
        pairs_ref[which] = ends[which] >> 1


def make_lists(place, cols, counts):
    most = cols.shape[0] * 24
    return pl.pallas_call(
        list_kernel,
        in_specs=[SMEM] * 3,
        out_specs=[SMEM] * 3,
        out_shape=[
            jax.ShapeDtypeStruct((LISTS, most + 2 * STEP), jnp.int32),
            jax.ShapeDtypeStruct((LISTS, most // 2 + STEP), jnp.int32),
            jax.ShapeDtypeStruct((2 * LISTS,), jnp.int32),
        ],
        name="make_lists",
    )(place, cols, counts)


def add_products(which, lists, blocks, panel, acc, first, end):
    order_ref, row_ref, pairs_ref = lists

    def one_step(step, carry):
        terms = []
        for pair in range(STEP):
            left, right = [], []
            for n in range(2):
                code = order_ref[which, (step * STEP + pair) * 2 + n]
                place, at = (code >> 8) & 31, code & 255
                row = row_ref[which, step * STEP + pair]
                left.append(jnp.concatenate([blocks[0, place, row], blocks[1, place, row]], axis=0))
                block = panel[at]
                right.append(jnp.where(code < SKIP, block, jnp.zeros_like(block)))
            terms.append(
                jnp.dot(
                    jnp.concatenate(left, axis=1),
                    jnp.concatenate(right, axis=0),
                    preferred_element_type=jnp.float32,
                )
            )
        for pair, term in enumerate(terms):
            acc[row_ref[which, step * STEP + pair]] += term
        return carry

    lax.fori_loop(first, end, one_step, 0)


def all_steps(which, lists):
    return (lists[2][which] + STEP - 1) // STEP


def run(which, lists, panel_parts, pieces, panel, blocks, acc, before, sems):
    half = blocks.shape[2] // 2
    early, at = [], 0
    for part in panel_parts:
        early.append((part, panel.at[pl.ds(at, part.shape[0])]))
        at += part.shape[0]
    if before is not None:
        early.append((before, acc))
    rounds = [early + split_pieces(pieces, blocks, 0, half), split_pieces(pieces, blocks, half, half)]
    copies, used = [], 0
    for pairs in rounds:
        copies.append([pltpu.make_async_copy(a, b, sems.at[used + n]) for n, (a, b) in enumerate(pairs)])
        used += len(pairs)
    for copy in copies[0] + copies[1]:
        copy.start()
    if before is None:
        acc[...] = jnp.zeros_like(acc)
    for copy in copies[0]:
        copy.wait()
    middle = lists[2][LISTS + which] // STEP
    add_products(which, lists, blocks, panel, acc, 0, middle)
    for copy in copies[1]:
        copy.wait()
    add_products(which, lists, blocks, panel, acc, middle, all_steps(which, lists))


def split_pieces(pieces, blocks, first, rows):
    pairs, at = [], 0
    lines = pl.ds(first, rows)
    for piece in pieces:
        if isinstance(piece, tuple):
            size = piece[0].shape[0]
            pairs += [(piece[n].at[:, lines], blocks.at[n, pl.ds(at, size), lines]) for n in range(2)]
        else:
            size = piece.shape[1]
            pairs.append((piece.at[:, :, lines], blocks.at[:, pl.ds(at, size), lines]))
        at += size
    return pairs


def early_kernel(order_ref, row_ref, pairs_ref, near, near_other, *refs):
    pieces, (acc, blocks, panel, sems) = refs[:8], refs[8:]
    lists = (order_ref, row_ref, pairs_ref)
    grouped = [*pieces[:3], (pieces[3], pieces[4]), *pieces[5:]]
    run(0, lists, [near, near_other], grouped, panel, blocks, acc, None, sems)


def main_kernel(order_ref, row_ref, pairs_ref, near, near_other, far, before, *refs):
    pieces, (blocks, acc, panel, sems) = refs[:12], refs[12:]
    lists = (order_ref, row_ref, pairs_ref)
    grouped = [*pieces[:3], (pieces[3], pieces[4]), *pieces[5:8], (pieces[8], pieces[9]), *pieces[10:]]
    run(1, lists, [near, near_other, far], grouped, panel, blocks, acc, before, sems)


def last_kernel(
    order_ref,
    row_ref,
    pairs_ref,
    panel,
    blocks,
    before,
    pert_real,
    pert_imag,
    drive_real,
    drive_imag,
    new_real,
    new_imag,
    acc,
):
    acc[...] = before[...]
    lists = (order_ref, row_ref, pairs_ref)
    add_products(2, lists, blocks, panel, acc, 0, all_steps(2, lists))

    def one_row(row, carry):
        total = acc[row]
        lines = pl.ds(row * BLOCK, BLOCK)
        ham_real, ham_imag = total[:BLOCK, :BLOCK], total[:BLOCK, BLOCK:]
        ovl_real, ovl_imag = total[BLOCK:, :BLOCK], total[BLOCK:, BLOCK:]
        res_real = drive_real[lines].astype(jnp.float32) - (
            ham_real - frequency * ovl_real + damping * ovl_imag
        )
        res_imag = drive_imag[lines].astype(jnp.float32) - (
            ham_imag - frequency * ovl_imag - damping * ovl_real
        )
        new_real[lines] = pert_real[lines].astype(jnp.float32) + step_length * res_real
        new_imag[lines] = pert_imag[lines].astype(jnp.float32) + step_length * res_imag
        return carry

    lax.fori_loop(0, acc.shape[0], one_row, 0)


SMEM = pl.BlockSpec(memory_space=pltpu.SMEM)
VMEM = pl.BlockSpec(memory_space=pltpu.VMEM)
ANY = pl.BlockSpec(memory_space=pl.ANY)


def nothing(*refs):
    pass


def after(array, *others):
    return pl.pallas_call(
        nothing,
        in_specs=[ANY] * (1 + len(others)),
        out_specs=ANY,
        out_shape=jax.ShapeDtypeStruct(array.shape, array.dtype),
        input_output_aliases={0: 0},
        compiler_params=pltpu.CompilerParams(vmem_limit_bytes=2**16),
        name="gate",
    )(in_hbm(array), *map(in_hbm, others))


def in_hbm(array):
    return pltpu.with_memory_space_constraint(array, pltpu.HBM)


def held(array):
    return pltpu.with_memory_space_constraint(array, pltpu.VMEM)


def cost(micros):
    return pl.CostEstimate(flops=0, bytes_accessed=int(micros * 3.0e6), transcendentals=0)


def early_products(lists, rows, panels, pieces):
    return pl.pallas_call(
        early_kernel,
        in_specs=[SMEM] * 3 + [ANY] * (2 + len(pieces)),
        out_specs=VMEM,
        out_shape=jax.ShapeDtypeStruct((rows, 2 * BLOCK, 2 * BLOCK), jnp.float32),
        scratch_shapes=[
            pltpu.VMEM((2, EARLY, rows, BLOCK, BLOCK), jnp.bfloat16),
            pltpu.VMEM((2 * panels[0].shape[0], BLOCK, 2 * BLOCK), jnp.bfloat16),
            pltpu.SemaphoreType.DMA((2 + 2 * len(pieces),)),
        ],
        compiler_params=pltpu.CompilerParams(vmem_limit_bytes=24 * 2**20),
        cost_estimate=cost(10),
        name="products_early",
    )(*lists, *map(in_hbm, panels), *map(in_hbm, pieces))


def main_products(lists, panels, before, pieces):
    rows = before.shape[0]
    args = [*panels, before, *pieces]
    return pl.pallas_call(
        main_kernel,
        in_specs=[SMEM] * 3 + [ANY] * len(args),
        out_specs=[VMEM, VMEM],
        out_shape=[
            pltpu.VMEM((2, 24, rows, BLOCK, BLOCK), jnp.bfloat16),
            pltpu.VMEM(before.shape, jnp.float32),
        ],
        scratch_shapes=[
            pltpu.VMEM((3 * panels[0].shape[0], BLOCK, 2 * BLOCK), jnp.bfloat16),
            pltpu.SemaphoreType.DMA((4 + 2 * len(pieces),)),
        ],
        compiler_params=pltpu.CompilerParams(vmem_limit_bytes=15 * 2**20),
        cost_estimate=cost(10),
        name="products_main",
    )(*lists, *map(in_hbm, args))


def last_products(lists, far_other, blocks, before, *flat):
    rows = before.shape[0]
    return pl.pallas_call(
        last_kernel,
        in_specs=[SMEM] * 3 + [VMEM] * 7,
        out_specs=[VMEM] * 2,
        out_shape=[jax.ShapeDtypeStruct((rows * BLOCK, BLOCK), jnp.float32)] * 2,
        scratch_shapes=[pltpu.VMEM(before.shape, jnp.float32)],
        compiler_params=pltpu.CompilerParams(vmem_limit_bytes=7 * 2**20),
        cost_estimate=cost(4),
        name="products_last",
    )(*lists, held(far_other), held(blocks), held(before), *flat)


def per_device(
    ham_blocks,
    margin_blocks,
    block_cols,
    block_counts,
    pert_real,
    pert_imag,
    drive_real,
    drive_imag,
):
    rows = block_cols.shape[0]
    place = jnp.stack([lax.axis_index(a) for a in ("ylo", "core", "x", "yhi")]).astype(jnp.int32)

    both = jnp.stack([ham_blocks.swapaxes(0, 1), margin_blocks.swapaxes(0, 1)], axis=0)
    panel = jnp.concatenate([pert_real, pert_imag], axis=1).reshape(rows, BLOCK, 2 * BLOCK)

    near = lax.all_gather(panel, "z", axis=0, tiled=True)
    from_left = shift(both, "x", 1)
    from_right = shift(both, "x", -1)
    part = shift(both[:, :2], "yhi")
    lists = make_lists(place, block_cols, block_counts)

    neighbour = shift(panel, "ylo")

    left_ham, right_margin = from_left[0], from_right[1]
    far = lax.all_gather(
        after(neighbour, left_ham, right_margin, part, lists[0]), "z", axis=0, tiled=True
    )
    part_left = shift(part, "x", 1)
    part_right = shift(part, "x", -1)
    far_ham = shift(left_ham, "x", 1)
    far_margin = shift(right_margin, "x", -1)
    late = shift(
        jnp.concatenate([both[:, 2:], from_left[:, 2:], from_right[:, 2:]], axis=1), "yhi"
    )

    near = after(near, part_left, part_right, far_ham, far_margin, late)
    near_other = shift(near, "core")
    part_far_ham = shift(part_left[0], "x", 1)
    part_far_margin = shift(part_right[1], "x", -1)
    late_far = shift(jnp.stack([far_ham[2:], far_margin[2:]], axis=0), "yhi")

    early = (both, from_left, from_right, far_ham, far_margin, part, part_left, part_right)
    pieces = early + (part_far_ham, part_far_margin, late, late_far)
    acc = early_products(lists, rows, (near, near_other), early)
    far = after(far, acc, part_far_ham, part_far_margin, late_far)
    far_other = shift(far, "core")
    blocks, acc = main_products(lists, (near, near_other, far), acc, pieces)
    new_real, new_imag = last_products(
        lists, far_other, blocks, acc, pert_real, pert_imag, drive_real, drive_imag
    )
    return new_real, new_imag


def solution(mesh):
    fine = jax.sharding.Mesh(mesh.devices.reshape(SIZES), AXES)
    loop, rep = ("ylo", "z", "core"), ("x", "yhi")
    return jax.shard_map(
        per_device,
        mesh=fine,
        in_specs=(
            P(loop, rep, None, None),
            P(loop, rep, None, None),
            P(loop, None),
            P(loop),
            P(loop, rep),
            P(loop, rep),
            P(loop, rep),
            P(loop, rep),
        ),
        out_specs=(P(loop, rep), P(loop, rep)),
        check_vma=False,
    )
```

```python
import jax
import jax.numpy as jnp
from jax import lax
from jax.experimental import pallas as pl
from jax.experimental.pallas import tpu as pltpu
from jax.sharding import PartitionSpec as P

frequency = 0.7
damping = 0.5
step_length = 0.5

AXES = ("ylo", "z", "core", "x", "yhi")
SIZES = (2, 8, 2, 4, 2)
BLOCK = 128


def moves(axis, by):
    place = AXES.index(axis)
    stride = 1
    for size in SIZES[place + 1 :]:
        stride *= size
    total = 1
    for size in SIZES:
        total *= size
    pairs = []
    for source in range(total):
        at = source // stride % SIZES[place]
        pairs.append((source, source + ((at + by) % SIZES[place] - at) * stride))
    return pairs


def shift(array, axis, by=1):
    return lax.ppermute(array, AXES, moves(axis, by))


PIECES = (
    (0, 0, (0, 1, 2)),
    (3, 0, (0, 1, 2)),
    (1, 0, (0, 1, 2)),
    (2, 0, (0, 1, 2)),
    (0, 1, (0, 1)),
    (3, 1, (0, 1)),
    (1, 1, (0, 1)),
    (2, 1, (0, 1)),
    (0, 1, (2,)),
    (3, 1, (2,)),
    (1, 1, (2,)),
    (2, 1, (2,)),
)
STEP = 4
EARLY = 18
LISTS = 3
SKIP = 2**16


def list_kernel(place_ref, cols_ref, counts_ref, order_ref, row_ref, pairs_ref):
    rows, slots = cols_ref.shape
    my_ylo, my_z, my_core, my_x, my_yhi = (place_ref[n] for n in range(5))

    def one_row(row, ends):
        for which in range(LISTS):
            pairs_ref[which] = ends[which]
        place = 0
        for dx, dy, local in PIECES:
            for j in local:
                slot = 3 * (2 * ((my_x + dx) & 3) + (my_yhi ^ dy)) + j
                column = cols_ref[row, slot]
                owner = column >> 3
                far = (owner >> 4) ^ my_ylo
                other = (owner & 1) ^ my_core
                ahead = ((owner >> 1) - my_z) & 7
                turn = jnp.where(ahead < 4, 2 * ahead, 15 - 2 * ahead)
                last = (turn + 2 * other >= 7).astype(jnp.int32)
                which = jnp.where(last == 1, 2, int(place >= EARLY))
                at = far * 8 + (column & 7)
                at += jnp.where(
                    last == 1,
                    jnp.where(other == 1, 16 * (turn - 4), 0),
                    16 * turn + jnp.where(turn >= 5, 80, 80 * (owner & 1)),
                )

                @pl.when(slot < counts_ref[row])
                def _(which=which, at=at, place=place):
                    n = pairs_ref[which]
                    order_ref[which, n] = place * 256 + at
                    row_ref[which, n >> 1] = row
                    pairs_ref[which] = n + 1

                place += 1
        out = []
        for which in range(LISTS):
            n = pairs_ref[which]
            order_ref[which, n] = SKIP
            out.append((n + 1) & ~1)
        return tuple(out)

    ends = lax.fori_loop(0, rows // 2, one_row, (0,) * LISTS)
    for which in range(LISTS):
        pairs_ref[LISTS + which] = ends[which] >> 1
    ends = lax.fori_loop(rows // 2, rows, one_row, ends)
    for which in range(LISTS):
        for n in range(2 * STEP):
            order_ref[which, ends[which] + n] = SKIP
        for n in range(STEP):
            row_ref[which, (ends[which] >> 1) + n] = rows - 1
        pairs_ref[which] = ends[which] >> 1


def make_lists(place, cols, counts):
    most = cols.shape[0] * 24
    return pl.pallas_call(
        list_kernel,
        in_specs=[SMEM] * 3,
        out_specs=[SMEM] * 3,
        out_shape=[
            jax.ShapeDtypeStruct((LISTS, most + 2 * STEP), jnp.int32),
            jax.ShapeDtypeStruct((LISTS, most // 2 + STEP), jnp.int32),
            jax.ShapeDtypeStruct((2 * LISTS,), jnp.int32),
        ],
        name="make_lists",
    )(place, cols, counts)


def add_products(which, lists, blocks, panel, acc, first, end):
    order_ref, row_ref, pairs_ref = lists

    def one_step(step, carry):
        terms = []
        for pair in range(STEP):
            left, right = [], []
            for n in range(2):
                code = order_ref[which, (step * STEP + pair) * 2 + n]
                place, at = (code >> 8) & 31, code & 255
                row = row_ref[which, step * STEP + pair]
                left.append(jnp.concatenate([blocks[0, place, row], blocks[1, place, row]], axis=0))
                block = panel[at]
                right.append(jnp.where(code < SKIP, block, jnp.zeros_like(block)))
            terms.append(
                jnp.dot(
                    jnp.concatenate(left, axis=1),
                    jnp.concatenate(right, axis=0),
                    preferred_element_type=jnp.float32,
                )
            )
        for pair, term in enumerate(terms):
            acc[row_ref[which, step * STEP + pair]] += term
        return carry

    lax.fori_loop(first, end, one_step, 0)


def all_steps(which, lists):
    return (lists[2][which] + STEP - 1) // STEP


def run(which, lists, panel_parts, pieces, panel, blocks, acc, before, sems):
    half = blocks.shape[2] // 2
    early, at = [], 0
    for part in panel_parts:
        early.append((part, panel.at[pl.ds(at, part.shape[0])]))
        at += part.shape[0]
    if before is not None:
        early.append((before, acc))
    rounds = [early + split_pieces(pieces, blocks, 0, half), split_pieces(pieces, blocks, half, half)]
    copies, used = [], 0
    for pairs in rounds:
        copies.append([pltpu.make_async_copy(a, b, sems.at[used + n]) for n, (a, b) in enumerate(pairs)])
        used += len(pairs)
    for copy in copies[0] + copies[1]:
        copy.start()
    if before is None:
        acc[...] = jnp.zeros_like(acc)
    for copy in copies[0]:
        copy.wait()
    middle = lists[2][LISTS + which] // STEP
    add_products(which, lists, blocks, panel, acc, 0, middle)
    for copy in copies[1]:
        copy.wait()
    add_products(which, lists, blocks, panel, acc, middle, all_steps(which, lists))


def split_pieces(pieces, blocks, first, rows):
    pairs, at = [], 0
    lines = pl.ds(first, rows)
    for piece in pieces:
        if isinstance(piece, tuple):
            size = piece[0].shape[0]
            pairs += [(piece[n].at[:, lines], blocks.at[n, pl.ds(at, size), lines]) for n in range(2)]
        else:
            size = piece.shape[1]
            pairs.append((piece.at[:, :, lines], blocks.at[:, pl.ds(at, size), lines]))
        at += size
    return pairs


def early_kernel(order_ref, row_ref, pairs_ref, *refs):
    parts, pieces, (acc, blocks, panel, sems) = refs[:3], refs[3:11], refs[11:]
    lists = (order_ref, row_ref, pairs_ref)
    grouped = [*pieces[:3], (pieces[3], pieces[4]), *pieces[5:]]
    run(0, lists, parts, grouped, panel, blocks, acc, None, sems)


def main_kernel(order_ref, row_ref, pairs_ref, *refs):
    parts, before, pieces = refs[:3], refs[3], refs[4:16]
    blocks, acc, panel, sems = refs[16:]
    lists = (order_ref, row_ref, pairs_ref)
    grouped = [*pieces[:3], (pieces[3], pieces[4]), *pieces[5:8], (pieces[8], pieces[9]), *pieces[10:]]
    run(1, lists, parts, grouped, panel, blocks, acc, before, sems)


def last_kernel(
    order_ref,
    row_ref,
    pairs_ref,
    end_up,
    end_down,
    other_end,
    blocks,
    before,
    pert_real,
    pert_imag,
    drive_real,
    drive_imag,
    new_real,
    new_imag,
    acc,
    panel,
    sems,
):
    copies, at = [], 0
    for n, part in enumerate((end_up, end_down, other_end)):
        copies.append(pltpu.make_async_copy(part, panel.at[pl.ds(at, part.shape[0])], sems.at[n]))
        at += part.shape[0]
    for copy in copies:
        copy.start()
    acc[...] = before[...]
    for copy in copies:
        copy.wait()
    lists = (order_ref, row_ref, pairs_ref)
    add_products(2, lists, blocks, panel, acc, 0, all_steps(2, lists))

    def one_row(row, carry):
        total = acc[row]
        lines = pl.ds(row * BLOCK, BLOCK)
        ham_real, ham_imag = total[:BLOCK, :BLOCK], total[:BLOCK, BLOCK:]
        ovl_real, ovl_imag = total[BLOCK:, :BLOCK], total[BLOCK:, BLOCK:]
        res_real = drive_real[lines].astype(jnp.float32) - (
            ham_real - frequency * ovl_real + damping * ovl_imag
        )
        res_imag = drive_imag[lines].astype(jnp.float32) - (
            ham_imag - frequency * ovl_imag - damping * ovl_real
        )
        new_real[lines] = pert_real[lines].astype(jnp.float32) + step_length * res_real
        new_imag[lines] = pert_imag[lines].astype(jnp.float32) + step_length * res_imag
        return carry

    lax.fori_loop(0, acc.shape[0], one_row, 0)


SMEM = pl.BlockSpec(memory_space=pltpu.SMEM)
VMEM = pl.BlockSpec(memory_space=pltpu.VMEM)
ANY = pl.BlockSpec(memory_space=pl.ANY)


def nothing(*refs):
    pass


def after(array, *others):
    return pl.pallas_call(
        nothing,
        in_specs=[ANY] * (1 + len(others)),
        out_specs=ANY,
        out_shape=jax.ShapeDtypeStruct(array.shape, array.dtype),
        input_output_aliases={0: 0},
        compiler_params=pltpu.CompilerParams(vmem_limit_bytes=2**16),
        name="gate",
    )(in_hbm(array), *map(in_hbm, others))


def in_hbm(array):
    return pltpu.with_memory_space_constraint(array, pltpu.HBM)


def pack_kernel(*refs):
    parts, out, sems = refs[:-2], refs[-2], refs[-1]
    copies, at = [], 0
    for n, part in enumerate(parts):
        copies.append(pltpu.make_async_copy(part, out.at[pl.ds(at, part.shape[0])], sems.at[n]))
        at += part.shape[0]
    for copy in copies:
        copy.start()
    for copy in copies:
        copy.wait()


def pack(parts):
    return pl.pallas_call(
        pack_kernel,
        in_specs=[ANY] * len(parts),
        out_specs=ANY,
        out_shape=jax.ShapeDtypeStruct((blocks_of(parts), BLOCK, 2 * BLOCK), jnp.bfloat16),
        scratch_shapes=[pltpu.SemaphoreType.DMA((len(parts),))],
        compiler_params=pltpu.CompilerParams(vmem_limit_bytes=2**16),
        cost_estimate=cost(3),
        name="pack",
    )(*map(in_hbm, parts))


def held(array):
    return pltpu.with_memory_space_constraint(array, pltpu.VMEM)


def cost(micros):
    return pl.CostEstimate(flops=0, bytes_accessed=int(micros * 3.0e6), transcendentals=0)


def blocks_of(parts):
    return sum(a.shape[0] for a in parts)


def early_products(lists, rows, parts, pieces):
    args = [*parts, *pieces]
    return pl.pallas_call(
        early_kernel,
        in_specs=[SMEM] * 3 + [ANY] * len(args),
        out_specs=VMEM,
        out_shape=jax.ShapeDtypeStruct((rows, 2 * BLOCK, 2 * BLOCK), jnp.float32),
        scratch_shapes=[
            pltpu.VMEM((2, EARLY, rows, BLOCK, BLOCK), jnp.bfloat16),
            pltpu.VMEM((blocks_of(parts), BLOCK, 2 * BLOCK), jnp.bfloat16),
            pltpu.SemaphoreType.DMA((len(parts) + 2 * len(pieces),)),
        ],
        compiler_params=pltpu.CompilerParams(vmem_limit_bytes=26 * 2**20),
        cost_estimate=cost(10),
        name="products_early",
    )(*lists, *map(in_hbm, args))


def main_products(lists, parts, before, pieces):
    args = [*parts, before, *pieces]
    return pl.pallas_call(
        main_kernel,
        in_specs=[SMEM] * 3 + [ANY] * len(args),
        out_specs=[VMEM, VMEM],
        out_shape=[
            pltpu.VMEM((2, 24, before.shape[0], BLOCK, BLOCK), jnp.bfloat16),
            pltpu.VMEM(before.shape, jnp.float32),
        ],
        scratch_shapes=[
            pltpu.VMEM((blocks_of(parts), BLOCK, 2 * BLOCK), jnp.bfloat16),
            pltpu.SemaphoreType.DMA((len(parts) + 1 + 2 * len(pieces),)),
        ],
        compiler_params=pltpu.CompilerParams(vmem_limit_bytes=15 * 2**20),
        cost_estimate=cost(10),
        name="products_main",
    )(*lists, *map(in_hbm, args))


def last_products(lists, parts, blocks, before, *flat):
    rows = before.shape[0]
    return pl.pallas_call(
        last_kernel,
        in_specs=[SMEM] * 3 + [ANY] * len(parts) + [VMEM] * 6,
        out_specs=[VMEM] * 2,
        out_shape=[jax.ShapeDtypeStruct((rows * BLOCK, BLOCK), jnp.float32)] * 2,
        scratch_shapes=[
            pltpu.VMEM(before.shape, jnp.float32),
            pltpu.VMEM((blocks_of(parts), BLOCK, 2 * BLOCK), jnp.bfloat16),
            pltpu.SemaphoreType.DMA((len(parts),)),
        ],
        compiler_params=pltpu.CompilerParams(vmem_limit_bytes=11 * 2**20),
        cost_estimate=cost(4),
        name="products_last",
    )(*lists, *parts, held(blocks), held(before), *flat)


def per_device(
    ham_blocks,
    margin_blocks,
    block_cols,
    block_counts,
    pert_real,
    pert_imag,
    drive_real,
    drive_imag,
):
    rows = block_cols.shape[0]
    place = jnp.stack([lax.axis_index(a) for a in ("ylo", "z", "core", "x", "yhi")]).astype(jnp.int32)

    both = jnp.stack([ham_blocks.swapaxes(0, 1), margin_blocks.swapaxes(0, 1)], axis=0)
    panel = jnp.concatenate([pert_real, pert_imag], axis=1).reshape(rows, BLOCK, 2 * BLOCK)

    from_left = shift(both, "x", 1)
    from_right = shift(both, "x", -1)
    neighbour = shift(panel, "ylo")
    own_up, own_down = shift(panel, "z", 1), shift(panel, "z", -1)

    part = shift(after(both[:, :2], neighbour), "yhi")
    up1 = jnp.concatenate([own_up, shift(neighbour, "z", 1)], axis=0)
    down1 = jnp.concatenate([own_down, shift(neighbour, "z", -1)], axis=0)

    far_ham = shift(from_left[0], "x", 1)
    far_margin = shift(from_right[1], "x", -1)
    up2, down2 = shift(up1, "z", 1), shift(down1, "z", -1)
    late = shift(
        after(jnp.concatenate([both[:, 2:], from_left[:, 2:], from_right[:, 2:]], axis=1), part),
        "yhi",
    )
    lists = make_lists(after(place, far_ham, far_margin), block_cols, block_counts)

    part_on = after(part, far_ham, far_margin)
    part_left = shift(part_on, "x", 1)
    part_right = shift(part_on, "x", -1)
    up3, down3 = shift(up2, "z", 1), shift(down2, "z", -1)
    come = (panel, neighbour, up1, down1, up2, down2)
    both_come = lax.all_to_all(pack(come + come), "core", 0, 0, tiled=True)
    late_far = shift(
        after(jnp.stack([far_ham[2:], far_margin[2:]], axis=0), late, part_left, part_right, lists[0], both_come),
        "yhi",
    )

    part_far_ham = shift(part_left[0], "x", 1)
    part_far_margin = shift(part_right[1], "x", -1)
    up3 = after(up3, part_left, part_right, late, both_come)
    down3 = after(down3, part_left, part_right, late, both_come)
    up4, down4 = shift(up3[:rows], "z", 1), shift(down3[rows:], "z", -1)

    early = (both, from_left, from_right, far_ham, far_margin, part_on, part_left, part_right)
    pieces = early + (part_far_ham, part_far_margin, late, late_far)
    panels = (both_come, up3, down3)
    acc = early_products(lists, rows, panels, early)
    other_end = shift(
        after(
            jnp.concatenate([up3, down3, up4, down4], axis=0),
            late_far,
            part_far_ham,
            part_far_margin,
            acc,
        ),
        "core",
    )
    blocks, acc = main_products(lists, panels, acc, pieces)
    new_real, new_imag = last_products(
        lists,
        (up4, down4, other_end),
        blocks,
        acc,
        pert_real,
        pert_imag,
        drive_real,
        drive_imag,
    )
    return new_real, new_imag


def solution(mesh):
    fine = jax.sharding.Mesh(mesh.devices.reshape(SIZES), AXES)
    loop, rep = ("ylo", "z", "core"), ("x", "yhi")
    return jax.shard_map(
        per_device,
        mesh=fine,
        in_specs=(
            P(loop, rep, None, None),
            P(loop, rep, None, None),
            P(loop, None),
            P(loop),
            P(loop, rep),
            P(loop, rep),
            P(loop, rep),
            P(loop, rep),
        ),
        out_specs=(P(loop, rep), P(loop, rep)),
        check_vma=False,
    )
```

```python
import jax
import jax.numpy as jnp
from jax import lax
from jax.experimental import pallas as pl
from jax.experimental.pallas import tpu as pltpu
from jax.sharding import PartitionSpec as P

frequency = 0.7
damping = 0.5
step_length = 0.5

AXES = ("ylo", "z", "core", "x", "yhi")
SIZES = (2, 8, 2, 4, 2)
BLOCK = 128


def moves(axis, by):
    place = AXES.index(axis)
    stride = 1
    for size in SIZES[place + 1 :]:
        stride *= size
    total = 1
    for size in SIZES:
        total *= size
    pairs = []
    for source in range(total):
        at = source // stride % SIZES[place]
        pairs.append((source, source + ((at + by) % SIZES[place] - at) * stride))
    return pairs


def shift(array, axis, by=1):
    return lax.ppermute(array, AXES, moves(axis, by))


PIECES = (
    (0, 0, (0, 1, 2)),
    (3, 0, (0, 1, 2)),
    (1, 0, (0, 1, 2)),
    (2, 0, (0, 1, 2)),
    (0, 1, (0, 1)),
    (3, 1, (0, 1)),
    (1, 1, (0, 1)),
    (2, 1, (0, 1)),
    (0, 1, (2,)),
    (3, 1, (2,)),
    (1, 1, (2,)),
    (2, 1, (2,)),
)
STEP = 4
EARLY = 18
LISTS = 3
SKIP = 2**16


def list_kernel(place_ref, cols_ref, counts_ref, order_ref, row_ref, pairs_ref):
    rows, slots = cols_ref.shape
    my_ylo, my_z, my_core, my_x, my_yhi = (place_ref[n] for n in range(5))

    def one_row(row, ends):
        for which in range(LISTS):
            pairs_ref[which] = ends[which]
        place = 0
        for dx, dy, local in PIECES:
            for j in local:
                slot = 3 * (2 * ((my_x + dx) & 3) + (my_yhi ^ dy)) + j
                column = cols_ref[row, slot]
                owner = column >> 3
                far = (owner >> 4) ^ my_ylo
                other = (owner & 1) ^ my_core
                ahead = ((owner >> 1) - my_z) & 7
                turn = jnp.where(ahead < 4, 2 * ahead, 15 - 2 * ahead)
                last = (turn + 2 * other >= 7).astype(jnp.int32)
                which = jnp.where(last == 1, 2, int(place >= EARLY))
                at = far * 8 + (column & 7)
                at += jnp.where(
                    last == 1,
                    jnp.where(other == 1, 16 * (turn - 4), 0),
                    16 * turn + jnp.where(turn >= 5, 80, 80 * (owner & 1)),
                )

                @pl.when(slot < counts_ref[row])
                def _(which=which, at=at, place=place):
                    n = pairs_ref[which]
                    order_ref[which, n] = place * 256 + at
                    row_ref[which, n >> 1] = row
                    pairs_ref[which] = n + 1

                place += 1
        out = []
        for which in range(LISTS):
            n = pairs_ref[which]
            order_ref[which, n] = SKIP
            out.append((n + 1) & ~1)
        return tuple(out)

    ends = lax.fori_loop(0, rows // 2, one_row, (0,) * LISTS)
    for which in range(LISTS):
        pairs_ref[LISTS + which] = ends[which] >> 1
    ends = lax.fori_loop(rows // 2, rows, one_row, ends)
    for which in range(LISTS):
        for n in range(2 * STEP):
            order_ref[which, ends[which] + n] = SKIP
        for n in range(STEP):
            row_ref[which, (ends[which] >> 1) + n] = rows - 1
        pairs_ref[which] = ends[which] >> 1


def make_lists(place, cols, counts):
    most = cols.shape[0] * 24
    return pl.pallas_call(
        list_kernel,
        in_specs=[SMEM] * 3,
        out_specs=[SMEM] * 3,
        out_shape=[
            jax.ShapeDtypeStruct((LISTS, most + 2 * STEP), jnp.int32),
            jax.ShapeDtypeStruct((LISTS, most // 2 + STEP), jnp.int32),
            jax.ShapeDtypeStruct((2 * LISTS,), jnp.int32),
        ],
        name="make_lists",
    )(place, cols, counts)


def add_products(which, lists, blocks, panel, acc, first, end):
    order_ref, row_ref, pairs_ref = lists

    def one_step(step, carry):
        terms = []
        for pair in range(STEP):
            left, right = [], []
            for n in range(2):
                code = order_ref[which, (step * STEP + pair) * 2 + n]
                place, at = (code >> 8) & 31, code & 255
                row = row_ref[which, step * STEP + pair]
                left.append(jnp.concatenate([blocks[0, place, row], blocks[1, place, row]], axis=0))
                block = panel[at]
                right.append(jnp.where(code < SKIP, block, jnp.zeros_like(block)))
            terms.append(
                jnp.dot(
                    jnp.concatenate(left, axis=1),
                    jnp.concatenate(right, axis=0),
                    preferred_element_type=jnp.float32,
                )
            )
        for pair, term in enumerate(terms):
            acc[row_ref[which, step * STEP + pair]] += term
        return carry

    lax.fori_loop(first, end, one_step, 0)


def all_steps(which, lists):
    return (lists[2][which] + STEP - 1) // STEP


def run(which, lists, early, pieces, offset, panel, blocks, acc, sems, fresh):
    half = blocks.shape[2] // 2
    rounds = [
        early + split_pieces(pieces, blocks, offset, 0, half),
        split_pieces(pieces, blocks, offset, half, half),
    ]
    copies, used = [], 0
    for pairs in rounds:
        copies.append([pltpu.make_async_copy(a, b, sems.at[used + n]) for n, (a, b) in enumerate(pairs)])
        used += len(pairs)
    for copy in copies[0] + copies[1]:
        copy.start()
    if fresh:
        acc[...] = jnp.zeros_like(acc)
    for copy in copies[0]:
        copy.wait()
    middle = lists[2][LISTS + which] // STEP
    add_products(which, lists, blocks, panel, acc, 0, middle)
    for copy in copies[1]:
        copy.wait()
    add_products(which, lists, blocks, panel, acc, middle, all_steps(which, lists))


def split_pieces(pieces, blocks, offset, first, rows):
    pairs, at = [], offset
    lines = pl.ds(first, rows)
    for piece in pieces:
        if isinstance(piece, tuple):
            size = piece[0].shape[0]
            pairs += [(piece[n].at[:, lines], blocks.at[n, pl.ds(at, size), lines]) for n in range(2)]
        else:
            size = piece.shape[1]
            pairs.append((piece.at[:, :, lines], blocks.at[:, pl.ds(at, size), lines]))
        at += size
    return pairs


def early_kernel(order_ref, row_ref, pairs_ref, *refs):
    parts, pieces, (panel, blocks, acc, token, sems) = refs[:3], refs[3:11], refs[11:]
    lists = (order_ref, row_ref, pairs_ref)
    early, at = [], 0
    for part in parts:
        early.append((part, panel.at[pl.ds(at, part.shape[0])]))
        at += part.shape[0]
    grouped = [*pieces[:3], (pieces[3], pieces[4]), *pieces[5:]]
    run(0, lists, early, grouped, 0, panel, blocks, acc, sems, True)
    token[...] = jnp.zeros_like(token)


def main_kernel(order_ref, row_ref, pairs_ref, panel, *refs):
    pieces, (blocks, acc, sems) = refs[2:6], refs[6:]
    lists = (order_ref, row_ref, pairs_ref)
    grouped = [(pieces[0], pieces[1]), *pieces[2:]]
    run(1, lists, [], grouped, EARLY, panel, blocks, acc, sems, False)


def last_kernel(
    order_ref,
    row_ref,
    pairs_ref,
    end_up,
    end_down,
    other_up,
    other_down,
    other_end,
    blocks,
    before,
    pert_real,
    pert_imag,
    drive_real,
    drive_imag,
    new_real,
    new_imag,
    acc,
    panel,
    sems,
):
    copies, at = [], 0
    for n, part in enumerate((end_up, end_down, other_up, other_down, other_end)):
        copies.append(pltpu.make_async_copy(part, panel.at[pl.ds(at, part.shape[0])], sems.at[n]))
        at += part.shape[0]
    for copy in copies:
        copy.start()
    acc[...] = before[...]
    for copy in copies:
        copy.wait()
    lists = (order_ref, row_ref, pairs_ref)
    add_products(2, lists, blocks, panel, acc, 0, all_steps(2, lists))

    def one_row(row, carry):
        total = acc[row]
        lines = pl.ds(row * BLOCK, BLOCK)
        ham_real, ham_imag = total[:BLOCK, :BLOCK], total[:BLOCK, BLOCK:]
        ovl_real, ovl_imag = total[BLOCK:, :BLOCK], total[BLOCK:, BLOCK:]
        res_real = drive_real[lines].astype(jnp.float32) - (
            ham_real - frequency * ovl_real + damping * ovl_imag
        )
        res_imag = drive_imag[lines].astype(jnp.float32) - (
            ham_imag - frequency * ovl_imag - damping * ovl_real
        )
        new_real[lines] = pert_real[lines].astype(jnp.float32) + step_length * res_real
        new_imag[lines] = pert_imag[lines].astype(jnp.float32) + step_length * res_imag
        return carry

    lax.fori_loop(0, acc.shape[0], one_row, 0)


SMEM = pl.BlockSpec(memory_space=pltpu.SMEM)
VMEM = pl.BlockSpec(memory_space=pltpu.VMEM)
ANY = pl.BlockSpec(memory_space=pl.ANY)


def nothing(*refs):
    pass


def after(array, *others):
    return pl.pallas_call(
        nothing,
        in_specs=[ANY] * (1 + len(others)),
        out_specs=ANY,
        out_shape=jax.ShapeDtypeStruct(array.shape, array.dtype),
        input_output_aliases={0: 0},
        compiler_params=pltpu.CompilerParams(vmem_limit_bytes=2**16),
        name="gate",
    )(in_hbm(array), *map(in_hbm, others))


def in_hbm(array):
    return pltpu.with_memory_space_constraint(array, pltpu.HBM)


def pack_kernel(*refs):
    parts, out, sems = refs[:-2], refs[-2], refs[-1]
    copies, at = [], 0
    for n, part in enumerate(parts):
        copies.append(pltpu.make_async_copy(part, out.at[pl.ds(at, part.shape[0])], sems.at[n]))
        at += part.shape[0]
    for copy in copies:
        copy.start()
    for copy in copies:
        copy.wait()


def pack(parts):
    return pl.pallas_call(
        pack_kernel,
        in_specs=[ANY] * len(parts),
        out_specs=ANY,
        out_shape=jax.ShapeDtypeStruct((blocks_of(parts), BLOCK, 2 * BLOCK), jnp.bfloat16),
        scratch_shapes=[pltpu.SemaphoreType.DMA((len(parts),))],
        compiler_params=pltpu.CompilerParams(vmem_limit_bytes=2**16),
        cost_estimate=cost(3),
        name="pack",
    )(*map(in_hbm, parts))


def held(array):
    return pltpu.with_memory_space_constraint(array, pltpu.VMEM)


def cost(micros):
    return pl.CostEstimate(flops=0, bytes_accessed=int(micros * 3.0e6), transcendentals=0)


def blocks_of(parts):
    return sum(a.shape[0] for a in parts)


def early_products(lists, rows, parts, pieces):
    args = [*parts, *pieces]
    return pl.pallas_call(
        early_kernel,
        in_specs=[SMEM] * 3 + [ANY] * len(args),
        out_specs=[VMEM] * 4,
        out_shape=[
            pltpu.VMEM((blocks_of(parts), BLOCK, 2 * BLOCK), jnp.bfloat16),
            pltpu.VMEM((2, 24, rows, BLOCK, BLOCK), jnp.bfloat16),
            pltpu.VMEM((rows, 2 * BLOCK, 2 * BLOCK), jnp.float32),
            jax.ShapeDtypeStruct((8, BLOCK), jnp.float32),
        ],
        scratch_shapes=[pltpu.SemaphoreType.DMA((len(parts) + 2 * len(pieces),))],
        compiler_params=pltpu.CompilerParams(vmem_limit_bytes=2 * 2**20),
        cost_estimate=cost(10),
        name="products_early",
    )(*lists, *map(in_hbm, args))


def main_products(lists, panel, blocks, before, pieces):
    return pl.pallas_call(
        main_kernel,
        in_specs=[SMEM] * 3 + [VMEM] * 3 + [ANY] * len(pieces),
        out_specs=[VMEM, VMEM],
        out_shape=[pltpu.VMEM(blocks.shape, blocks.dtype), pltpu.VMEM(before.shape, before.dtype)],
        scratch_shapes=[pltpu.SemaphoreType.DMA((2 * len(pieces),))],
        input_output_aliases={4: 0, 5: 1},
        compiler_params=pltpu.CompilerParams(vmem_limit_bytes=2 * 2**20),
        cost_estimate=cost(4),
        name="products_main",
    )(*lists, held(panel), held(blocks), held(before), *map(in_hbm, pieces))


def last_products(lists, parts, blocks, before, *flat):
    rows = before.shape[0]
    return pl.pallas_call(
        last_kernel,
        in_specs=[SMEM] * 3 + [ANY] * len(parts) + [VMEM] * 6,
        out_specs=[VMEM] * 2,
        out_shape=[jax.ShapeDtypeStruct((rows * BLOCK, BLOCK), jnp.float32)] * 2,
        scratch_shapes=[
            pltpu.VMEM(before.shape, jnp.float32),
            pltpu.VMEM((blocks_of(parts), BLOCK, 2 * BLOCK), jnp.bfloat16),
            pltpu.SemaphoreType.DMA((len(parts),)),
        ],
        compiler_params=pltpu.CompilerParams(vmem_limit_bytes=11 * 2**20),
        cost_estimate=cost(4),
        name="products_last",
    )(*lists, *parts, held(blocks), held(before), *flat)


def per_device(
    ham_blocks,
    margin_blocks,
    block_cols,
    block_counts,
    pert_real,
    pert_imag,
    drive_real,
    drive_imag,
):
    rows = block_cols.shape[0]
    place = jnp.stack([lax.axis_index(a) for a in ("ylo", "z", "core", "x", "yhi")]).astype(jnp.int32)

    both = jnp.stack([ham_blocks.swapaxes(0, 1), margin_blocks.swapaxes(0, 1)], axis=0)
    panel = jnp.concatenate([pert_real, pert_imag], axis=1).reshape(rows, BLOCK, 2 * BLOCK)

    from_left = shift(both, "x", 1)
    from_right = shift(both, "x", -1)
    neighbour = shift(panel, "ylo")
    own_up, own_down = shift(panel, "z", 1), shift(panel, "z", -1)

    part = shift(after(both[:, :2], neighbour), "yhi")
    up1 = jnp.concatenate([own_up, shift(neighbour, "z", 1)], axis=0)
    down1 = jnp.concatenate([own_down, shift(neighbour, "z", -1)], axis=0)

    far_ham = shift(from_left[0], "x", 1)
    far_margin = shift(from_right[1], "x", -1)
    up2, down2 = shift(up1, "z", 1), shift(down1, "z", -1)
    late = shift(
        after(jnp.concatenate([both[:, 2:], from_left[:, 2:], from_right[:, 2:]], axis=1), part),
        "yhi",
    )
    lists = make_lists(after(place, far_ham, far_margin), block_cols, block_counts)

    part_on = after(part, far_ham, far_margin)
    part_left = shift(part_on, "x", 1)
    part_right = shift(part_on, "x", -1)
    up3, down3 = shift(up2, "z", 1), shift(down2, "z", -1)
    come = (panel, neighbour, up1, down1, up2, down2)
    both_come = lax.all_to_all(pack(come + come), "core", 0, 0, tiled=True)
    late_far = shift(
        after(jnp.stack([far_ham[2:], far_margin[2:]], axis=0), late, part_left, part_right, lists[0], both_come),
        "yhi",
    )

    part_far_ham = shift(part_left[0], "x", 1)
    part_far_margin = shift(part_right[1], "x", -1)
    up3 = after(up3, part_left, part_right, late, both_come)
    down3 = after(down3, part_left, part_right, late, both_come)
    up4, down4 = shift(up3[:rows], "z", 1), shift(down3[rows:], "z", -1)

    early = (both, from_left, from_right, far_ham, far_margin, part_on, part_left, part_right)
    kept, blocks, acc, token = early_products(lists, rows, (both_come, up3, down3), early)
    other_up = shift(after(up3, late_far, part_far_ham, part_far_margin, token), "core")
    other_down = shift(after(down3, late_far, part_far_ham, part_far_margin, token), "core")
    other_end = shift(jnp.concatenate([up4, down4], axis=0), "core")
    late_ones = (part_far_ham, part_far_margin, late, late_far)
    blocks, acc = main_products(lists, kept, blocks, acc, late_ones)
    new_real, new_imag = last_products(
        lists,
        (up4, down4, other_up, other_down, other_end),
        blocks,
        acc,
        pert_real,
        pert_imag,
        drive_real,
        drive_imag,
    )
    return new_real, new_imag


def solution(mesh):
    fine = jax.sharding.Mesh(mesh.devices.reshape(SIZES), AXES)
    loop, rep = ("ylo", "z", "core"), ("x", "yhi")
    return jax.shard_map(
        per_device,
        mesh=fine,
        in_specs=(
            P(loop, rep, None, None),
            P(loop, rep, None, None),
            P(loop, None),
            P(loop),
            P(loop, rep),
            P(loop, rep),
            P(loop, rep),
            P(loop, rep),
        ),
        out_specs=(P(loop, rep), P(loop, rep)),
        check_vma=False,
    )
```

```python
import jax
import jax.numpy as jnp
from jax import lax
from jax.experimental import pallas as pl
from jax.experimental.pallas import tpu as pltpu
from jax.sharding import PartitionSpec as P

frequency = 0.7
damping = 0.5
step_length = 0.5

AXES = ("ylo", "z", "core", "x", "yhi")
SIZES = (2, 8, 2, 4, 2)
BLOCK = 128


def moves(axis, by):
    place = AXES.index(axis)
    stride = 1
    for size in SIZES[place + 1 :]:
        stride *= size
    total = 1
    for size in SIZES:
        total *= size
    pairs = []
    for source in range(total):
        at = source // stride % SIZES[place]
        pairs.append((source, source + ((at + by) % SIZES[place] - at) * stride))
    return pairs


def shift(array, axis, by=1):
    return lax.ppermute(array, AXES, moves(axis, by))


PIECES = (
    (0, 0, (0, 1, 2)),
    (3, 0, (0, 1, 2)),
    (1, 0, (0, 1, 2)),
    (2, 0, (0, 1, 2)),
    (0, 1, (0, 1)),
    (3, 1, (0, 1)),
    (1, 1, (0, 1)),
    (2, 1, (0, 1)),
    (0, 1, (2,)),
    (3, 1, (2,)),
    (1, 1, (2,)),
    (2, 1, (2,)),
)
STEP = 4
EARLY = 18
LISTS = 3
SKIP = 2**16


def list_kernel(place_ref, cols_ref, counts_ref, order_ref, row_ref, pairs_ref):
    rows, slots = cols_ref.shape
    my_ylo, my_z, my_core, my_x, my_yhi = (place_ref[n] for n in range(5))

    def one_row(row, ends):
        for which in range(LISTS):
            pairs_ref[which] = ends[which]
        place = 0
        for dx, dy, local in PIECES:
            for j in local:
                slot = 3 * (2 * ((my_x + dx) & 3) + (my_yhi ^ dy)) + j
                column = cols_ref[row, slot]
                owner = column >> 3
                far = (owner >> 4) ^ my_ylo
                other = (owner & 1) ^ my_core
                ahead = ((owner >> 1) - my_z) & 7
                turn = jnp.where(ahead < 4, 2 * ahead, 15 - 2 * ahead)
                last = (turn + 2 * other >= 7).astype(jnp.int32)
                which = jnp.where(last == 1, 2, int(place >= EARLY))
                at = far * 8 + (column & 7)
                at += jnp.where(
                    last == 1,
                    jnp.where(other == 1, 16 * (turn - 4), 0),
                    16 * turn + jnp.where(turn >= 5, 80, 80 * (owner & 1)),
                )

                @pl.when(slot < counts_ref[row])
                def _(which=which, at=at, place=place):
                    n = pairs_ref[which]
                    order_ref[which, n] = place * 256 + at
                    row_ref[which, n >> 1] = row
                    pairs_ref[which] = n + 1

                place += 1
        out = []
        for which in range(LISTS):
            n = pairs_ref[which]
            order_ref[which, n] = SKIP
            out.append((n + 1) & ~1)
        return tuple(out)

    ends = lax.fori_loop(0, rows // 2, one_row, (0,) * LISTS)
    for which in range(LISTS):
        pairs_ref[LISTS + which] = ends[which] >> 1
    ends = lax.fori_loop(rows // 2, rows, one_row, ends)
    for which in range(LISTS):
        for n in range(2 * STEP):
            order_ref[which, ends[which] + n] = SKIP
        for n in range(STEP):
            row_ref[which, (ends[which] >> 1) + n] = rows - 1
        pairs_ref[which] = ends[which] >> 1


def make_lists(place, cols, counts):
    most = cols.shape[0] * 24
    return pl.pallas_call(
        list_kernel,
        in_specs=[SMEM] * 3,
        out_specs=[SMEM] * 3,
        out_shape=[
            jax.ShapeDtypeStruct((LISTS, most + 2 * STEP), jnp.int32),
            jax.ShapeDtypeStruct((LISTS, most // 2 + STEP), jnp.int32),
            jax.ShapeDtypeStruct((2 * LISTS,), jnp.int32),
        ],
        name="make_lists",
    )(place, cols, counts)


def add_products(which, lists, blocks, panel, acc, first, end):
    order_ref, row_ref, pairs_ref = lists

    def one_step(step, carry):
        terms = []
        for pair in range(STEP):
            left, right = [], []
            for n in range(2):
                code = order_ref[which, (step * STEP + pair) * 2 + n]
                place, at = (code >> 8) & 31, code & 255
                row = row_ref[which, step * STEP + pair]
                left.append(jnp.concatenate([blocks[0, place, row], blocks[1, place, row]], axis=0))
                block = panel[at]
                right.append(jnp.where(code < SKIP, block, jnp.zeros_like(block)))
            terms.append(
                jnp.dot(
                    jnp.concatenate(left, axis=1),
                    jnp.concatenate(right, axis=0),
                    preferred_element_type=jnp.float32,
                )
            )
        for pair, term in enumerate(terms):
            acc[row_ref[which, step * STEP + pair]] += term
        return carry

    lax.fori_loop(first, end, one_step, 0)


def all_steps(which, lists):
    return (lists[2][which] + STEP - 1) // STEP


def run(which, lists, early, pieces, offset, panel, blocks, acc, sems, fresh):
    half = blocks.shape[2] // 2
    rounds = [
        early + split_pieces(pieces, blocks, offset, 0, half),
        split_pieces(pieces, blocks, offset, half, half),
    ]
    copies, used = [], 0
    for pairs in rounds:
        copies.append([pltpu.make_async_copy(a, b, sems.at[used + n]) for n, (a, b) in enumerate(pairs)])
        used += len(pairs)
    for copy in copies[0] + copies[1]:
        copy.start()
    if fresh:
        acc[...] = jnp.zeros_like(acc)
    for copy in copies[0]:
        copy.wait()
    middle = lists[2][LISTS + which] // STEP
    add_products(which, lists, blocks, panel, acc, 0, middle)
    for copy in copies[1]:
        copy.wait()
    add_products(which, lists, blocks, panel, acc, middle, all_steps(which, lists))


def split_pieces(pieces, blocks, offset, first, rows):
    pairs, at = [], offset
    lines = pl.ds(first, rows)
    for piece in pieces:
        if isinstance(piece, tuple):
            size = piece[0].shape[0]
            pairs += [(piece[n].at[:, lines], blocks.at[n, pl.ds(at, size), lines]) for n in range(2)]
        else:
            size = piece.shape[1]
            pairs.append((piece.at[:, :, lines], blocks.at[:, pl.ds(at, size), lines]))
        at += size
    return pairs


def early_kernel(order_ref, row_ref, pairs_ref, *refs):
    parts, pieces, (panel, blocks, acc, token, sems) = refs[:3], refs[3:11], refs[11:]
    lists = (order_ref, row_ref, pairs_ref)
    early, at = [], 0
    for part in parts:
        early.append((part, panel.at[pl.ds(at, part.shape[0])]))
        at += part.shape[0]
    grouped = [*pieces[:3], (pieces[3], pieces[4]), *pieces[5:]]
    run(0, lists, early, grouped, 0, panel, blocks, acc, sems, True)
    token[...] = jnp.zeros_like(token)


def main_kernel(order_ref, row_ref, pairs_ref, panel, *refs):
    pieces, (blocks, acc, sems) = refs[2:6], refs[6:]
    lists = (order_ref, row_ref, pairs_ref)
    grouped = [(pieces[0], pieces[1]), *pieces[2:]]
    run(1, lists, [], grouped, EARLY, panel, blocks, acc, sems, False)


def last_kernel(
    order_ref,
    row_ref,
    pairs_ref,
    end_up,
    end_down,
    other_up,
    other_down,
    other_end,
    blocks,
    before,
    pert_real,
    pert_imag,
    drive_real,
    drive_imag,
    new_real,
    new_imag,
    acc,
    panel,
    sems,
):
    copies, at = [], 0
    for n, part in enumerate((end_up, end_down, other_up, other_down, other_end)):
        copies.append(pltpu.make_async_copy(part, panel.at[pl.ds(at, part.shape[0])], sems.at[n]))
        at += part.shape[0]
    for copy in copies:
        copy.start()
    acc[...] = before[...]
    for copy in copies:
        copy.wait()
    lists = (order_ref, row_ref, pairs_ref)
    add_products(2, lists, blocks, panel, acc, 0, all_steps(2, lists))

    def one_row(row, carry):
        total = acc[row]
        lines = pl.ds(row * BLOCK, BLOCK)
        ham_real, ham_imag = total[:BLOCK, :BLOCK], total[:BLOCK, BLOCK:]
        ovl_real, ovl_imag = total[BLOCK:, :BLOCK], total[BLOCK:, BLOCK:]
        res_real = drive_real[lines].astype(jnp.float32) - (
            ham_real - frequency * ovl_real + damping * ovl_imag
        )
        res_imag = drive_imag[lines].astype(jnp.float32) - (
            ham_imag - frequency * ovl_imag - damping * ovl_real
        )
        new_real[lines] = pert_real[lines].astype(jnp.float32) + step_length * res_real
        new_imag[lines] = pert_imag[lines].astype(jnp.float32) + step_length * res_imag
        return carry

    lax.fori_loop(0, acc.shape[0], one_row, 0)


SMEM = pl.BlockSpec(memory_space=pltpu.SMEM)
VMEM = pl.BlockSpec(memory_space=pltpu.VMEM)
ANY = pl.BlockSpec(memory_space=pl.ANY)


def nothing(*refs):
    pass


def after(array, *others):
    return pl.pallas_call(
        nothing,
        in_specs=[ANY] * (1 + len(others)),
        out_specs=ANY,
        out_shape=jax.ShapeDtypeStruct(array.shape, array.dtype),
        input_output_aliases={0: 0},
        compiler_params=pltpu.CompilerParams(vmem_limit_bytes=2**16),
        name="gate",
    )(in_hbm(array), *map(in_hbm, others))


def in_hbm(array):
    return pltpu.with_memory_space_constraint(array, pltpu.HBM)


def pack_kernel(*refs):
    parts, out, sems = refs[:-2], refs[-2], refs[-1]
    copies, at = [], 0
    for n, part in enumerate(parts):
        copies.append(pltpu.make_async_copy(part, out.at[pl.ds(at, part.shape[0])], sems.at[n]))
        at += part.shape[0]
    for copy in copies:
        copy.start()
    for copy in copies:
        copy.wait()


def pack(parts):
    return pl.pallas_call(
        pack_kernel,
        in_specs=[ANY] * len(parts),
        out_specs=ANY,
        out_shape=pltpu.HBM((blocks_of(parts), BLOCK, 2 * BLOCK), jnp.bfloat16),
        scratch_shapes=[pltpu.SemaphoreType.DMA((len(parts),))],
        compiler_params=pltpu.CompilerParams(vmem_limit_bytes=2**16),
        cost_estimate=cost(3),
        name="pack",
    )(*map(in_hbm, parts))


def held(array):
    return pltpu.with_memory_space_constraint(array, pltpu.VMEM)


def cost(micros):
    return pl.CostEstimate(flops=0, bytes_accessed=int(micros * 3.0e6), transcendentals=0)


def blocks_of(parts):
    return sum(a.shape[0] for a in parts)


def early_products(lists, rows, parts, pieces):
    args = [*parts, *pieces]
    return pl.pallas_call(
        early_kernel,
        in_specs=[SMEM] * 3 + [ANY] * len(args),
        out_specs=[VMEM] * 4,
        out_shape=[
            pltpu.VMEM((blocks_of(parts), BLOCK, 2 * BLOCK), jnp.bfloat16),
            pltpu.VMEM((2, 24, rows, BLOCK, BLOCK), jnp.bfloat16),
            pltpu.VMEM((rows, 2 * BLOCK, 2 * BLOCK), jnp.float32),
            jax.ShapeDtypeStruct((8, BLOCK), jnp.float32),
        ],
        scratch_shapes=[pltpu.SemaphoreType.DMA((len(parts) + 2 * len(pieces),))],
        compiler_params=pltpu.CompilerParams(vmem_limit_bytes=2 * 2**20),
        cost_estimate=cost(10),
        name="products_early",
    )(*lists, *map(in_hbm, args))


def main_products(lists, panel, blocks, before, pieces):
    return pl.pallas_call(
        main_kernel,
        in_specs=[SMEM] * 3 + [VMEM] * 3 + [ANY] * len(pieces),
        out_specs=[VMEM, VMEM],
        out_shape=[pltpu.VMEM(blocks.shape, blocks.dtype), pltpu.VMEM(before.shape, before.dtype)],
        scratch_shapes=[pltpu.SemaphoreType.DMA((2 * len(pieces),))],
        input_output_aliases={4: 0, 5: 1},
        compiler_params=pltpu.CompilerParams(vmem_limit_bytes=2 * 2**20),
        cost_estimate=cost(4),
        name="products_main",
    )(*lists, held(panel), held(blocks), held(before), *map(in_hbm, pieces))


def last_products(lists, parts, blocks, before, *flat):
    rows = before.shape[0]
    return pl.pallas_call(
        last_kernel,
        in_specs=[SMEM] * 3 + [ANY] * len(parts) + [VMEM] * 6,
        out_specs=[VMEM] * 2,
        out_shape=[jax.ShapeDtypeStruct((rows * BLOCK, BLOCK), jnp.float32)] * 2,
        scratch_shapes=[
            pltpu.VMEM(before.shape, jnp.float32),
            pltpu.VMEM((blocks_of(parts), BLOCK, 2 * BLOCK), jnp.bfloat16),
            pltpu.SemaphoreType.DMA((len(parts),)),
        ],
        compiler_params=pltpu.CompilerParams(vmem_limit_bytes=11 * 2**20),
        cost_estimate=cost(4),
        name="products_last",
    )(*lists, *parts, held(blocks), held(before), *flat)


def per_device(
    ham_blocks,
    margin_blocks,
    block_cols,
    block_counts,
    pert_real,
    pert_imag,
    drive_real,
    drive_imag,
):
    rows = block_cols.shape[0]
    place = jnp.stack([lax.axis_index(a) for a in ("ylo", "z", "core", "x", "yhi")]).astype(jnp.int32)

    both = jnp.stack([ham_blocks.swapaxes(0, 1), margin_blocks.swapaxes(0, 1)], axis=0)
    panel = jnp.concatenate([pert_real, pert_imag], axis=1).reshape(rows, BLOCK, 2 * BLOCK)

    from_left = shift(both, "x", 1)
    from_right = shift(both, "x", -1)
    neighbour = shift(panel, "ylo")
    own_up, own_down = shift(panel, "z", 1), shift(panel, "z", -1)

    part = shift(after(both[:, :2], neighbour, own_up, own_down), "yhi")
    up1 = jnp.concatenate([own_up, shift(neighbour, "z", 1)], axis=0)
    down1 = jnp.concatenate([own_down, shift(neighbour, "z", -1)], axis=0)

    far_ham = shift(from_left[0], "x", 1)
    far_margin = shift(from_right[1], "x", -1)
    up2, down2 = shift(up1, "z", 1), shift(down1, "z", -1)
    late = shift(
        after(jnp.concatenate([both[:, 2:], from_left[:, 2:], from_right[:, 2:]], axis=1), part),
        "yhi",
    )
    lists = make_lists(after(place, neighbour), block_cols, block_counts)

    part_on = after(part, far_ham, far_margin)
    part_left = shift(part_on, "x", 1)
    part_right = shift(part_on, "x", -1)
    up3, down3 = shift(up2, "z", 1), shift(down2, "z", -1)
    come = (panel, neighbour, up1, down1, up2, down2)
    both_come = lax.all_to_all(pack(come + come), "core", 0, 0, tiled=True)
    part_far_ham = shift(part_left[0], "x", 1)
    part_far_margin = shift(part_right[1], "x", -1)
    late_far = shift(
        after(jnp.stack([far_ham[2:], far_margin[2:]], axis=0), late, part_far_ham, part_far_margin, lists[0], both_come),
        "yhi",
    )

    up3 = after(up3, part_left, part_right, late, both_come)
    down3 = after(down3, part_left, part_right, late, both_come)
    up4, down4 = shift(up3[:rows], "z", 1), shift(down3[rows:], "z", -1)

    early = (both, from_left, from_right, far_ham, far_margin, part_on, part_left, part_right)
    kept, blocks, acc, token = early_products(lists, rows, (both_come, up3, down3), early)
    other_up = shift(after(up3, late_far, part_far_ham, part_far_margin, token), "core")
    other_down = shift(after(down3, late_far, part_far_ham, part_far_margin, token), "core")
    other_end = shift(jnp.concatenate([up4, down4], axis=0), "core")
    late_ones = (part_far_ham, part_far_margin, late, late_far)
    blocks, acc = main_products(lists, kept, blocks, acc, late_ones)
    new_real, new_imag = last_products(
        lists,
        (up4, down4, other_up, other_down, other_end),
        blocks,
        acc,
        pert_real,
        pert_imag,
        drive_real,
        drive_imag,
    )
    return new_real, new_imag


def solution(mesh):
    fine = jax.sharding.Mesh(mesh.devices.reshape(SIZES), AXES)
    loop, rep = ("ylo", "z", "core"), ("x", "yhi")
    return jax.shard_map(
        per_device,
        mesh=fine,
        in_specs=(
            P(loop, rep, None, None),
            P(loop, rep, None, None),
            P(loop, None),
            P(loop),
            P(loop, rep),
            P(loop, rep),
            P(loop, rep),
            P(loop, rep),
        ),
        out_specs=(P(loop, rep), P(loop, rep)),
        check_vma=False,
    )
```

```python
import jax
import jax.numpy as jnp
from jax import lax
from jax.experimental import pallas as pl
from jax.experimental.pallas import tpu as pltpu
from jax.sharding import PartitionSpec as P

frequency = 0.7
damping = 0.5
step_length = 0.5

AXES = ("ylo", "z", "core", "x", "yhi")
SIZES = (2, 8, 2, 4, 2)
BLOCK = 128


def moves(axis, by):
    place = AXES.index(axis)
    stride = 1
    for size in SIZES[place + 1 :]:
        stride *= size
    total = 1
    for size in SIZES:
        total *= size
    pairs = []
    for source in range(total):
        at = source // stride % SIZES[place]
        pairs.append((source, source + ((at + by) % SIZES[place] - at) * stride))
    return pairs


def shift(array, axis, by=1):
    return lax.ppermute(array, AXES, moves(axis, by))


PIECES = (
    (0, 0, (0, 1, 2)),
    (3, 0, (0, 1, 2)),
    (1, 0, (0, 1, 2)),
    (2, 0, (0, 1, 2)),
    (0, 1, (0, 1)),
    (3, 1, (0, 1)),
    (1, 1, (0, 1)),
    (2, 1, (0, 1)),
    (0, 1, (2,)),
    (3, 1, (2,)),
    (1, 1, (2,)),
    (2, 1, (2,)),
)
STEP = 4
EARLY = 18
LISTS = 3
SKIP = 2**16


def list_kernel(place_ref, cols_ref, counts_ref, order_ref, row_ref, pairs_ref):
    rows, slots = cols_ref.shape
    my_ylo, my_z, my_core, my_x, my_yhi = (place_ref[n] for n in range(5))

    def one_row(row, ends):
        for which in range(LISTS):
            pairs_ref[which] = ends[which]
        place = 0
        for dx, dy, local in PIECES:
            for j in local:
                slot = 3 * (2 * ((my_x + dx) & 3) + (my_yhi ^ dy)) + j
                column = cols_ref[row, slot]
                owner = column >> 3
                far = (owner >> 4) ^ my_ylo
                other = (owner & 1) ^ my_core
                ahead = ((owner >> 1) - my_z) & 7
                turn = jnp.where(ahead < 4, 2 * ahead, 15 - 2 * ahead)
                last = (turn + 2 * other >= 7).astype(jnp.int32)
                which = jnp.where(last == 1, 2, int(place >= EARLY))
                at = far * 8 + (column & 7)
                at += jnp.where(
                    last == 1,
                    jnp.where(other == 1, 16 * (turn - 4), 0),
                    16 * turn + jnp.where(turn >= 5, 80, 80 * (owner & 1)),
                )

                @pl.when(slot < counts_ref[row])
                def _(which=which, at=at, place=place):
                    n = pairs_ref[which]
                    order_ref[which, n] = place * 256 + at
                    row_ref[which, n >> 1] = row
                    pairs_ref[which] = n + 1

                place += 1
        out = []
        for which in range(LISTS):
            n = pairs_ref[which]
            order_ref[which, n] = SKIP
            out.append((n + 1) & ~1)
        return tuple(out)

    ends = lax.fori_loop(0, rows // 2, one_row, (0,) * LISTS)
    for which in range(LISTS):
        pairs_ref[LISTS + which] = ends[which] >> 1
    ends = lax.fori_loop(rows // 2, rows, one_row, ends)
    for which in range(LISTS):
        for n in range(2 * STEP):
            order_ref[which, ends[which] + n] = SKIP
        for n in range(STEP):
            row_ref[which, (ends[which] >> 1) + n] = rows - 1
        pairs_ref[which] = ends[which] >> 1


def make_lists(place, cols, counts):
    most = cols.shape[0] * 24
    return pl.pallas_call(
        list_kernel,
        in_specs=[SMEM] * 3,
        out_specs=[SMEM] * 3,
        out_shape=[
            jax.ShapeDtypeStruct((LISTS, most + 2 * STEP), jnp.int32),
            jax.ShapeDtypeStruct((LISTS, most // 2 + STEP), jnp.int32),
            jax.ShapeDtypeStruct((2 * LISTS,), jnp.int32),
        ],
        name="make_lists",
    )(place, cols, counts)


def add_products(which, lists, blocks, panel, acc, first, end):
    order_ref, row_ref, pairs_ref = lists

    def one_step(step, carry):
        terms = []
        for pair in range(STEP):
            left, right = [], []
            for n in range(2):
                code = order_ref[which, (step * STEP + pair) * 2 + n]
                place, at = (code >> 8) & 31, code & 255
                row = row_ref[which, step * STEP + pair]
                left.append(jnp.concatenate([blocks[0, place, row], blocks[1, place, row]], axis=0))
                block = panel[at]
                right.append(jnp.where(code < SKIP, block, jnp.zeros_like(block)))
            terms.append(
                jnp.dot(
                    jnp.concatenate(left, axis=1),
                    jnp.concatenate(right, axis=0),
                    preferred_element_type=jnp.float32,
                )
            )
        for pair, term in enumerate(terms):
            acc[row_ref[which, step * STEP + pair]] += term
        return carry

    lax.fori_loop(first, end, one_step, 0)


def all_steps(which, lists):
    return (lists[2][which] + STEP - 1) // STEP


def run(which, lists, early, pieces, offset, panel, blocks, acc, sems, fresh):
    half = blocks.shape[2] // 2
    rounds = [
        early + split_pieces(pieces, blocks, offset, 0, half),
        split_pieces(pieces, blocks, offset, half, half),
    ]
    copies, used = [], 0
    for pairs in rounds:
        copies.append([pltpu.make_async_copy(a, b, sems.at[used + n]) for n, (a, b) in enumerate(pairs)])
        used += len(pairs)
    for copy in copies[0] + copies[1]:
        copy.start()
    if fresh:
        acc[...] = jnp.zeros_like(acc)
    for copy in copies[0]:
        copy.wait()
    middle = lists[2][LISTS + which] // STEP
    add_products(which, lists, blocks, panel, acc, 0, middle)
    for copy in copies[1]:
        copy.wait()
    add_products(which, lists, blocks, panel, acc, middle, all_steps(which, lists))


def split_pieces(pieces, blocks, offset, first, rows):
    pairs, at = [], offset
    lines = pl.ds(first, rows)
    for piece in pieces:
        if isinstance(piece, tuple):
            size = piece[0].shape[0]
            pairs += [(piece[n].at[:, lines], blocks.at[n, pl.ds(at, size), lines]) for n in range(2)]
        else:
            size = piece.shape[1]
            pairs.append((piece.at[:, :, lines], blocks.at[:, pl.ds(at, size), lines]))
        at += size
    return pairs


def early_kernel(order_ref, row_ref, pairs_ref, *refs):
    parts, pieces, (panel, blocks, acc, token, sems) = refs[:3], refs[3:11], refs[11:]
    lists = (order_ref, row_ref, pairs_ref)
    early, at = [], 0
    for part in parts:
        early.append((part, panel.at[pl.ds(at, part.shape[0])]))
        at += part.shape[0]
    grouped = [*pieces[:3], (pieces[3], pieces[4]), *pieces[5:]]
    run(0, lists, early, grouped, 0, panel, blocks, acc, sems, True)
    token[...] = jnp.zeros_like(token)


def main_kernel(order_ref, row_ref, pairs_ref, panel, *refs):
    pieces, (blocks, acc, sems) = refs[2:6], refs[6:]
    lists = (order_ref, row_ref, pairs_ref)
    grouped = [(pieces[0], pieces[1]), *pieces[2:]]
    run(1, lists, [], grouped, EARLY, panel, blocks, acc, sems, False)


def last_kernel(
    order_ref,
    row_ref,
    pairs_ref,
    end_up,
    end_down,
    other_up,
    other_down,
    other_end,
    blocks,
    before,
    pert_real,
    pert_imag,
    drive_real,
    drive_imag,
    new_real,
    new_imag,
    acc,
    panel,
    sems,
):
    copies, at = [], 0
    for n, part in enumerate((end_up, end_down, other_up, other_down, other_end)):
        copies.append(pltpu.make_async_copy(part, panel.at[pl.ds(at, part.shape[0])], sems.at[n]))
        at += part.shape[0]
    for copy in copies:
        copy.start()
    acc[...] = before[...]
    for copy in copies:
        copy.wait()
    lists = (order_ref, row_ref, pairs_ref)
    add_products(2, lists, blocks, panel, acc, 0, all_steps(2, lists))

    def one_row(row, carry):
        total = acc[row]
        lines = pl.ds(row * BLOCK, BLOCK)
        ham_real, ham_imag = total[:BLOCK, :BLOCK], total[:BLOCK, BLOCK:]
        ovl_real, ovl_imag = total[BLOCK:, :BLOCK], total[BLOCK:, BLOCK:]
        res_real = drive_real[lines].astype(jnp.float32) - (
            ham_real - frequency * ovl_real + damping * ovl_imag
        )
        res_imag = drive_imag[lines].astype(jnp.float32) - (
            ham_imag - frequency * ovl_imag - damping * ovl_real
        )
        new_real[lines] = pert_real[lines].astype(jnp.float32) + step_length * res_real
        new_imag[lines] = pert_imag[lines].astype(jnp.float32) + step_length * res_imag
        return carry

    lax.fori_loop(0, acc.shape[0], one_row, 0)


SMEM = pl.BlockSpec(memory_space=pltpu.SMEM)
VMEM = pl.BlockSpec(memory_space=pltpu.VMEM)
ANY = pl.BlockSpec(memory_space=pl.ANY)


def nothing(*refs):
    pass


def after(array, *others):
    return pl.pallas_call(
        nothing,
        in_specs=[ANY] * (1 + len(others)),
        out_specs=ANY,
        out_shape=jax.ShapeDtypeStruct(array.shape, array.dtype),
        input_output_aliases={0: 0},
        compiler_params=pltpu.CompilerParams(vmem_limit_bytes=2**16),
        name="gate",
    )(in_hbm(array), *map(in_hbm, others))


def in_hbm(array):
    return pltpu.with_memory_space_constraint(array, pltpu.HBM)


def pack_kernel(*refs):
    parts, (out, whole, sems) = refs[:-3], refs[-3:]
    count = whole.shape[0]
    copies, at = [], 0
    for n, part in enumerate(parts):
        copies.append(pltpu.make_async_copy(part, whole.at[pl.ds(at, part.shape[0])], sems.at[n]))
        at += part.shape[0]
    for copy in copies:
        copy.start()
    for copy in copies:
        copy.wait()
    halves = [
        pltpu.make_async_copy(whole, out.at[pl.ds(n * count, count)], sems.at[len(parts) + n])
        for n in range(2)
    ]
    for copy in halves:
        copy.start()
    for copy in halves:
        copy.wait()


def pack_twice(parts):
    count = blocks_of(parts)
    return pl.pallas_call(
        pack_kernel,
        in_specs=[ANY] * len(parts),
        out_specs=ANY,
        out_shape=pltpu.HBM((2 * count, BLOCK, 2 * BLOCK), jnp.bfloat16),
        scratch_shapes=[
            pltpu.VMEM((count, BLOCK, 2 * BLOCK), jnp.bfloat16),
            pltpu.SemaphoreType.DMA((len(parts) + 2,)),
        ],
        compiler_params=pltpu.CompilerParams(vmem_limit_bytes=6 * 2**20),
        cost_estimate=cost(4),
        name="pack",
    )(*map(in_hbm, parts))


def held(array):
    return pltpu.with_memory_space_constraint(array, pltpu.VMEM)


def cost(micros):
    return pl.CostEstimate(flops=0, bytes_accessed=int(micros * 3.0e6), transcendentals=0)


def blocks_of(parts):
    return sum(a.shape[0] for a in parts)


def early_products(lists, rows, parts, pieces):
    args = [*parts, *pieces]
    return pl.pallas_call(
        early_kernel,
        in_specs=[SMEM] * 3 + [ANY] * len(args),
        out_specs=[VMEM] * 4,
        out_shape=[
            pltpu.VMEM((blocks_of(parts), BLOCK, 2 * BLOCK), jnp.bfloat16),
            pltpu.VMEM((2, 24, rows, BLOCK, BLOCK), jnp.bfloat16),
            pltpu.VMEM((rows, 2 * BLOCK, 2 * BLOCK), jnp.float32),
            jax.ShapeDtypeStruct((8, BLOCK), jnp.float32),
        ],
        scratch_shapes=[pltpu.SemaphoreType.DMA((len(parts) + 2 * len(pieces),))],
        compiler_params=pltpu.CompilerParams(vmem_limit_bytes=2 * 2**20),
        cost_estimate=cost(10),
        name="products_early",
    )(*lists, *map(in_hbm, args))


def main_products(lists, panel, blocks, before, pieces):
    return pl.pallas_call(
        main_kernel,
        in_specs=[SMEM] * 3 + [VMEM] * 3 + [ANY] * len(pieces),
        out_specs=[VMEM, VMEM],
        out_shape=[pltpu.VMEM(blocks.shape, blocks.dtype), pltpu.VMEM(before.shape, before.dtype)],
        scratch_shapes=[pltpu.SemaphoreType.DMA((2 * len(pieces),))],
        input_output_aliases={4: 0, 5: 1},
        compiler_params=pltpu.CompilerParams(vmem_limit_bytes=2 * 2**20),
        cost_estimate=cost(4),
        name="products_main",
    )(*lists, held(panel), held(blocks), held(before), *map(in_hbm, pieces))


def last_products(lists, parts, blocks, before, *flat):
    rows = before.shape[0]
    return pl.pallas_call(
        last_kernel,
        in_specs=[SMEM] * 3 + [ANY] * len(parts) + [VMEM] * 6,
        out_specs=[VMEM] * 2,
        out_shape=[jax.ShapeDtypeStruct((rows * BLOCK, BLOCK), jnp.float32)] * 2,
        scratch_shapes=[
            pltpu.VMEM(before.shape, jnp.float32),
            pltpu.VMEM((blocks_of(parts), BLOCK, 2 * BLOCK), jnp.bfloat16),
            pltpu.SemaphoreType.DMA((len(parts),)),
        ],
        compiler_params=pltpu.CompilerParams(vmem_limit_bytes=11 * 2**20),
        cost_estimate=cost(4),
        name="products_last",
    )(*lists, *parts, held(blocks), held(before), *flat)


def per_device(
    ham_blocks,
    margin_blocks,
    block_cols,
    block_counts,
    pert_real,
    pert_imag,
    drive_real,
    drive_imag,
):
    rows = block_cols.shape[0]
    place = jnp.stack([lax.axis_index(a) for a in ("ylo", "z", "core", "x", "yhi")]).astype(jnp.int32)

    both = jnp.stack([ham_blocks.swapaxes(0, 1), margin_blocks.swapaxes(0, 1)], axis=0)
    panel = jnp.concatenate([pert_real, pert_imag], axis=1).reshape(rows, BLOCK, 2 * BLOCK)

    from_left = shift(both, "x", 1)
    from_right = shift(both, "x", -1)
    neighbour = shift(panel, "ylo")
    own_up, own_down = shift(panel, "z", 1), shift(panel, "z", -1)

    lists = make_lists(place, block_cols, block_counts)
    part = shift(after(both[:, :2], neighbour, own_up, own_down, lists[0]), "yhi")
    up1 = jnp.concatenate([own_up, shift(neighbour, "z", 1)], axis=0)
    down1 = jnp.concatenate([own_down, shift(neighbour, "z", -1)], axis=0)

    far_ham = shift(from_left[0], "x", 1)
    far_margin = shift(from_right[1], "x", -1)
    up2, down2 = shift(up1, "z", 1), shift(down1, "z", -1)
    late = shift(
        after(jnp.concatenate([both[:, 2:], from_left[:, 2:], from_right[:, 2:]], axis=1), part),
        "yhi",
    )

    part_on = after(part, far_ham, far_margin)
    part_left = shift(part_on, "x", 1)
    part_right = shift(part_on, "x", -1)
    up3, down3 = shift(up2, "z", 1), shift(down2, "z", -1)
    come = (panel, neighbour, up1, down1, up2, down2)
    both_come = lax.all_to_all(pack_twice(come), "core", 0, 0, tiled=True)
    part_far_ham = shift(part_left[0], "x", 1)
    part_far_margin = shift(part_right[1], "x", -1)
    late_far = shift(
        after(jnp.stack([far_ham[2:], far_margin[2:]], axis=0), late, part_far_ham, part_far_margin, lists[0], both_come),
        "yhi",
    )

    up3 = after(up3, part_left, part_right, late, both_come)
    down3 = after(down3, part_left, part_right, late, both_come)
    up4, down4 = shift(up3[:rows], "z", 1), shift(down3[rows:], "z", -1)

    early = (both, from_left, from_right, far_ham, far_margin, part_on, part_left, part_right)
    kept, blocks, acc, token = early_products(lists, rows, (both_come, up3, down3), early)
    other_up = shift(after(up3, late_far, part_far_ham, part_far_margin, token), "core")
    other_down = shift(after(down3, late_far, part_far_ham, part_far_margin, token), "core")
    other_end = shift(jnp.concatenate([up4, down4], axis=0), "core")
    late_ones = (part_far_ham, part_far_margin, late, late_far)
    blocks, acc = main_products(lists, kept, blocks, acc, late_ones)
    new_real, new_imag = last_products(
        lists,
        (up4, down4, other_up, other_down, other_end),
        blocks,
        acc,
        pert_real,
        pert_imag,
        drive_real,
        drive_imag,
    )
    return new_real, new_imag


def solution(mesh):
    fine = jax.sharding.Mesh(mesh.devices.reshape(SIZES), AXES)
    loop, rep = ("ylo", "z", "core"), ("x", "yhi")
    return jax.shard_map(
        per_device,
        mesh=fine,
        in_specs=(
            P(loop, rep, None, None),
            P(loop, rep, None, None),
            P(loop, None),
            P(loop),
            P(loop, rep),
            P(loop, rep),
            P(loop, rep),
            P(loop, rep),
        ),
        out_specs=(P(loop, rep), P(loop, rep)),
        check_vma=False,
    )
```

```python
import jax
import jax.numpy as jnp
from jax import lax
from jax.experimental import pallas as pl
from jax.experimental.pallas import tpu as pltpu
from jax.sharding import PartitionSpec as P

frequency = 0.7
damping = 0.5
step_length = 0.5

AXES = ("ylo", "z", "core", "x", "yhi")
SIZES = (2, 8, 2, 4, 2)
BLOCK = 128


def moves(axis, by):
    place = AXES.index(axis)
    stride = 1
    for size in SIZES[place + 1 :]:
        stride *= size
    total = 1
    for size in SIZES:
        total *= size
    pairs = []
    for source in range(total):
        at = source // stride % SIZES[place]
        pairs.append((source, source + ((at + by) % SIZES[place] - at) * stride))
    return pairs


def shift(array, axis, by=1):
    return lax.ppermute(array, AXES, moves(axis, by))


PIECES = (
    (0, 0, (0, 1, 2)),
    (3, 0, (0, 1, 2)),
    (1, 0, (0, 1, 2)),
    (2, 0, (0, 1, 2)),
    (0, 1, (0, 1)),
    (3, 1, (0, 1)),
    (1, 1, (0, 1)),
    (2, 1, (0, 1)),
    (0, 1, (2,)),
    (3, 1, (2,)),
    (1, 1, (2,)),
    (2, 1, (2,)),
)
STEP = 4
EARLY = 18
LISTS = 3
SKIP = 2**16


def list_kernel(place_ref, cols_ref, counts_ref, order_ref, row_ref, pairs_ref):
    rows, slots = cols_ref.shape
    my_ylo, my_z, my_core, my_x, my_yhi = (place_ref[n] for n in range(5))

    def one_row(row, ends):
        for which in range(LISTS):
            pairs_ref[which] = ends[which]
        place = 0
        for dx, dy, local in PIECES:
            for j in local:
                slot = 3 * (2 * ((my_x + dx) & 3) + (my_yhi ^ dy)) + j
                column = cols_ref[row, slot]
                owner = column >> 3
                far = (owner >> 4) ^ my_ylo
                other = (owner & 1) ^ my_core
                ahead = ((owner >> 1) - my_z) & 7
                turn = jnp.where(ahead < 4, 2 * ahead, 15 - 2 * ahead)
                last = (turn + 2 * other >= 7).astype(jnp.int32)
                which = jnp.where(last == 1, 2, int(place >= EARLY))
                at = far * 8 + (column & 7)
                at += jnp.where(
                    last == 1,
                    jnp.where(other == 1, 16 * (turn - 4), 0),
                    16 * turn + jnp.where(turn >= 5, 80, 80 * (owner & 1)),
                )

                @pl.when(slot < counts_ref[row])
                def _(which=which, at=at, place=place):
                    n = pairs_ref[which]
                    order_ref[which, n] = place * 256 + at
                    row_ref[which, n >> 1] = row
                    pairs_ref[which] = n + 1

                place += 1
        out = []
        for which in range(LISTS):
            n = pairs_ref[which]
            order_ref[which, n] = SKIP
            out.append((n + 1) & ~1)
        return tuple(out)

    ends = lax.fori_loop(0, rows // 2, one_row, (0,) * LISTS)
    for which in range(LISTS):
        pairs_ref[LISTS + which] = ends[which] >> 1
    ends = lax.fori_loop(rows // 2, rows, one_row, ends)
    for which in range(LISTS):
        for n in range(2 * STEP):
            order_ref[which, ends[which] + n] = SKIP
        for n in range(STEP):
            row_ref[which, (ends[which] >> 1) + n] = rows - 1
        pairs_ref[which] = ends[which] >> 1


def make_lists(place, cols, counts):
    most = cols.shape[0] * 24
    return pl.pallas_call(
        list_kernel,
        in_specs=[SMEM] * 3,
        out_specs=[SMEM] * 3,
        out_shape=[
            jax.ShapeDtypeStruct((LISTS, most + 2 * STEP), jnp.int32),
            jax.ShapeDtypeStruct((LISTS, most // 2 + STEP), jnp.int32),
            jax.ShapeDtypeStruct((2 * LISTS,), jnp.int32),
        ],
        name="make_lists",
    )(place, cols, counts)


def add_products(which, lists, blocks, panel, acc, first, end):
    order_ref, row_ref, pairs_ref = lists

    def one_step(step, carry):
        terms = []
        for pair in range(STEP):
            left, right = [], []
            for n in range(2):
                code = order_ref[which, (step * STEP + pair) * 2 + n]
                place, at = (code >> 8) & 31, code & 255
                row = row_ref[which, step * STEP + pair]
                left.append(jnp.concatenate([blocks[0, place, row], blocks[1, place, row]], axis=0))
                block = panel[at]
                right.append(jnp.where(code < SKIP, block, jnp.zeros_like(block)))
            terms.append(
                jnp.dot(
                    jnp.concatenate(left, axis=1),
                    jnp.concatenate(right, axis=0),
                    preferred_element_type=jnp.float32,
                )
            )
        for pair, term in enumerate(terms):
            acc[row_ref[which, step * STEP + pair]] += term
        return carry

    lax.fori_loop(first, end, one_step, 0)


def all_steps(which, lists):
    return (lists[2][which] + STEP - 1) // STEP


def run(which, lists, early, pieces, offset, panel, blocks, acc, sems, fresh):
    half = blocks.shape[2] // 2
    rounds = [
        early + split_pieces(pieces, blocks, offset, 0, half),
        split_pieces(pieces, blocks, offset, half, half),
    ]
    copies, used = [], 0
    for pairs in rounds:
        copies.append([pltpu.make_async_copy(a, b, sems.at[used + n]) for n, (a, b) in enumerate(pairs)])
        used += len(pairs)
    for copy in copies[0] + copies[1]:
        copy.start()
    if fresh:
        acc[...] = jnp.zeros_like(acc)
    for copy in copies[0]:
        copy.wait()
    middle = lists[2][LISTS + which] // STEP
    add_products(which, lists, blocks, panel, acc, 0, middle)
    for copy in copies[1]:
        copy.wait()
    add_products(which, lists, blocks, panel, acc, middle, all_steps(which, lists))


def split_pieces(pieces, blocks, offset, first, rows):
    pairs, at = [], offset
    lines = pl.ds(first, rows)
    for piece in pieces:
        if isinstance(piece, tuple):
            size = piece[0].shape[0]
            pairs += [(piece[n].at[:, lines], blocks.at[n, pl.ds(at, size), lines]) for n in range(2)]
        else:
            size = piece.shape[1]
            pairs.append((piece.at[:, :, lines], blocks.at[:, pl.ds(at, size), lines]))
        at += size
    return pairs


def early_kernel(order_ref, row_ref, pairs_ref, *refs):
    parts, pieces, (panel, blocks, acc, token, sems) = refs[:3], refs[3:11], refs[11:]
    lists = (order_ref, row_ref, pairs_ref)
    early, at = [], 0
    for part in parts:
        early.append((part, panel.at[pl.ds(at, part.shape[0])]))
        at += part.shape[0]
    grouped = [*pieces[:3], (pieces[3], pieces[4]), *pieces[5:]]
    run(0, lists, early, grouped, 0, panel, blocks, acc, sems, True)
    token[...] = jnp.zeros_like(token)


def main_kernel(order_ref, row_ref, pairs_ref, panel, *refs):
    pieces, (blocks, acc, sems) = refs[2:6], refs[6:]
    lists = (order_ref, row_ref, pairs_ref)
    grouped = [(pieces[0], pieces[1]), *pieces[2:]]
    run(1, lists, [], grouped, EARLY, panel, blocks, acc, sems, False)


def last_kernel(
    order_ref,
    row_ref,
    pairs_ref,
    end_up,
    end_down,
    other_up,
    other_down,
    other_end,
    blocks,
    before,
    pert_real,
    pert_imag,
    drive_real,
    drive_imag,
    new_real,
    new_imag,
    acc,
    panel,
    sems,
):
    copies, at = [], 0
    for n, part in enumerate((end_up, end_down, other_up, other_down, other_end)):
        copies.append(pltpu.make_async_copy(part, panel.at[pl.ds(at, part.shape[0])], sems.at[n]))
        at += part.shape[0]
    for copy in copies:
        copy.start()
    acc[...] = before[...]
    for copy in copies:
        copy.wait()
    lists = (order_ref, row_ref, pairs_ref)
    add_products(2, lists, blocks, panel, acc, 0, all_steps(2, lists))

    def one_row(row, carry):
        total = acc[row]
        lines = pl.ds(row * BLOCK, BLOCK)
        ham_real, ham_imag = total[:BLOCK, :BLOCK], total[:BLOCK, BLOCK:]
        ovl_real, ovl_imag = total[BLOCK:, :BLOCK], total[BLOCK:, BLOCK:]
        res_real = drive_real[lines].astype(jnp.float32) - (
            ham_real - frequency * ovl_real + damping * ovl_imag
        )
        res_imag = drive_imag[lines].astype(jnp.float32) - (
            ham_imag - frequency * ovl_imag - damping * ovl_real
        )
        new_real[lines] = pert_real[lines].astype(jnp.float32) + step_length * res_real
        new_imag[lines] = pert_imag[lines].astype(jnp.float32) + step_length * res_imag
        return carry

    lax.fori_loop(0, acc.shape[0], one_row, 0)


SMEM = pl.BlockSpec(memory_space=pltpu.SMEM)
VMEM = pl.BlockSpec(memory_space=pltpu.VMEM)
ANY = pl.BlockSpec(memory_space=pl.ANY)


def nothing(*refs):
    pass


def after(array, *others):
    return pl.pallas_call(
        nothing,
        in_specs=[ANY] * (1 + len(others)),
        out_specs=ANY,
        out_shape=jax.ShapeDtypeStruct(array.shape, array.dtype),
        input_output_aliases={0: 0},
        compiler_params=pltpu.CompilerParams(vmem_limit_bytes=2**16),
        name="gate",
    )(in_hbm(array), *map(in_hbm, others))


def in_hbm(array):
    return pltpu.with_memory_space_constraint(array, pltpu.HBM)


def pack_kernel(*refs):
    parts, (out, whole, sems) = refs[:-3], refs[-3:]
    count = whole.shape[0]
    copies, at = [], 0
    for n, part in enumerate(parts):
        copies.append(pltpu.make_async_copy(part, whole.at[pl.ds(at, part.shape[0])], sems.at[n]))
        at += part.shape[0]
    for copy in copies:
        copy.start()
    for copy in copies:
        copy.wait()
    halves = [
        pltpu.make_async_copy(whole, out.at[pl.ds(n * count, count)], sems.at[len(parts) + n])
        for n in range(2)
    ]
    for copy in halves:
        copy.start()
    for copy in halves:
        copy.wait()


def pack_twice(parts):
    count = blocks_of(parts)
    return pl.pallas_call(
        pack_kernel,
        in_specs=[ANY] * len(parts),
        out_specs=ANY,
        out_shape=pltpu.HBM((2 * count, BLOCK, 2 * BLOCK), jnp.bfloat16),
        scratch_shapes=[
            pltpu.VMEM((count, BLOCK, 2 * BLOCK), jnp.bfloat16),
            pltpu.SemaphoreType.DMA((len(parts) + 2,)),
        ],
        compiler_params=pltpu.CompilerParams(vmem_limit_bytes=6 * 2**20),
        cost_estimate=cost(4),
        name="pack",
    )(*map(in_hbm, parts))


def held(array):
    return pltpu.with_memory_space_constraint(array, pltpu.VMEM)


def cost(micros):
    return pl.CostEstimate(flops=0, bytes_accessed=int(micros * 3.0e6), transcendentals=0)


def blocks_of(parts):
    return sum(a.shape[0] for a in parts)


def early_products(lists, rows, parts, pieces):
    args = [*parts, *pieces]
    return pl.pallas_call(
        early_kernel,
        in_specs=[SMEM] * 3 + [ANY] * len(args),
        out_specs=[VMEM] * 4,
        out_shape=[
            pltpu.VMEM((blocks_of(parts), BLOCK, 2 * BLOCK), jnp.bfloat16),
            pltpu.VMEM((2, 24, rows, BLOCK, BLOCK), jnp.bfloat16),
            pltpu.VMEM((rows, 2 * BLOCK, 2 * BLOCK), jnp.float32),
            jax.ShapeDtypeStruct((8, BLOCK), jnp.float32),
        ],
        scratch_shapes=[pltpu.SemaphoreType.DMA((len(parts) + 2 * len(pieces),))],
        compiler_params=pltpu.CompilerParams(vmem_limit_bytes=2 * 2**20),
        cost_estimate=cost(10),
        name="products_early",
    )(*lists, *map(in_hbm, args))


def main_products(lists, panel, blocks, before, pieces):
    return pl.pallas_call(
        main_kernel,
        in_specs=[SMEM] * 3 + [VMEM] * 3 + [ANY] * len(pieces),
        out_specs=[VMEM, VMEM],
        out_shape=[pltpu.VMEM(blocks.shape, blocks.dtype), pltpu.VMEM(before.shape, before.dtype)],
        scratch_shapes=[pltpu.SemaphoreType.DMA((2 * len(pieces),))],
        input_output_aliases={4: 0, 5: 1},
        compiler_params=pltpu.CompilerParams(vmem_limit_bytes=2 * 2**20),
        cost_estimate=cost(4),
        name="products_main",
    )(*lists, held(panel), held(blocks), held(before), *map(in_hbm, pieces))


def last_products(lists, parts, blocks, before, *flat):
    rows = before.shape[0]
    return pl.pallas_call(
        last_kernel,
        in_specs=[SMEM] * 3 + [ANY] * len(parts) + [VMEM] * 6,
        out_specs=[VMEM] * 2,
        out_shape=[jax.ShapeDtypeStruct((rows * BLOCK, BLOCK), jnp.float32)] * 2,
        scratch_shapes=[
            pltpu.VMEM(before.shape, jnp.float32),
            pltpu.VMEM((blocks_of(parts), BLOCK, 2 * BLOCK), jnp.bfloat16),
            pltpu.SemaphoreType.DMA((len(parts),)),
        ],
        compiler_params=pltpu.CompilerParams(vmem_limit_bytes=11 * 2**20),
        cost_estimate=cost(4),
        name="products_last",
    )(*lists, *parts, held(blocks), held(before), *flat)


def per_device(
    ham_blocks,
    margin_blocks,
    block_cols,
    block_counts,
    pert_real,
    pert_imag,
    drive_real,
    drive_imag,
):
    rows = block_cols.shape[0]
    place = jnp.stack([lax.axis_index(a) for a in ("ylo", "z", "core", "x", "yhi")]).astype(jnp.int32)

    both = jnp.stack([ham_blocks.swapaxes(0, 1), margin_blocks.swapaxes(0, 1)], axis=0)
    panel = jnp.concatenate([pert_real, pert_imag], axis=1).reshape(rows, BLOCK, 2 * BLOCK)

    from_left = shift(both, "x", 1)
    from_right = shift(both, "x", -1)
    neighbour = shift(panel, "ylo")
    own_up, own_down = shift(panel, "z", 1), shift(panel, "z", -1)

    lists = make_lists(place, block_cols, block_counts)
    part = shift(after(both[:, :2], neighbour), "yhi")
    up1 = jnp.concatenate([own_up, shift(neighbour, "z", 1)], axis=0)
    down1 = jnp.concatenate([own_down, shift(neighbour, "z", -1)], axis=0)

    far_ham = shift(after(from_left[0], up1), "x", 1)
    far_margin = shift(after(from_right[1], down1), "x", -1)
    up2, down2 = shift(up1, "z", 1), shift(down1, "z", -1)
    late = shift(
        after(
            jnp.concatenate([both[:, 2:], from_left[:, 2:], from_right[:, 2:]], axis=1),
            part,
            lists[0],
        ),
        "yhi",
    )

    part_on = after(part, far_ham, far_margin)
    part_left = shift(part_on, "x", 1)
    part_right = shift(part_on, "x", -1)
    up3, down3 = shift(up2, "z", 1), shift(down2, "z", -1)
    come = (panel, neighbour, up1, down1, up2, down2)
    both_come = lax.all_to_all(pack_twice(come), "core", 0, 0, tiled=True)
    part_far_ham = shift(part_left[0], "x", 1)
    part_far_margin = shift(part_right[1], "x", -1)
    late_far = shift(
        after(jnp.stack([far_ham[2:], far_margin[2:]], axis=0), late, part_far_ham, part_far_margin, lists[0], both_come),
        "yhi",
    )

    up3 = after(up3, part_left, part_right, both_come)
    down3 = after(down3, part_left, part_right, both_come)
    up4, down4 = shift(up3[:rows], "z", 1), shift(down3[rows:], "z", -1)

    early = (both, from_left, from_right, far_ham, far_margin, part_on, part_left, part_right)
    kept, blocks, acc, token = early_products(lists, rows, (both_come, up3, down3), early)
    other_up = shift(after(up3, late_far, part_far_ham, part_far_margin, token), "core")
    other_down = shift(after(down3, late_far, part_far_ham, part_far_margin, token), "core")
    other_end = shift(jnp.concatenate([up4, down4], axis=0), "core")
    late_ones = (part_far_ham, part_far_margin, late, late_far)
    blocks, acc = main_products(lists, kept, blocks, acc, late_ones)
    new_real, new_imag = last_products(
        lists,
        (up4, down4, other_up, other_down, other_end),
        blocks,
        acc,
        pert_real,
        pert_imag,
        drive_real,
        drive_imag,
    )
    return new_real, new_imag


def solution(mesh):
    fine = jax.sharding.Mesh(mesh.devices.reshape(SIZES), AXES)
    loop, rep = ("ylo", "z", "core"), ("x", "yhi")
    return jax.shard_map(
        per_device,
        mesh=fine,
        in_specs=(
            P(loop, rep, None, None),
            P(loop, rep, None, None),
            P(loop, None),
            P(loop),
            P(loop, rep),
            P(loop, rep),
            P(loop, rep),
            P(loop, rep),
        ),
        out_specs=(P(loop, rep), P(loop, rep)),
        check_vma=False,
    )
```
